256 devices in a mesh: branch: 2 (over y_hi), strip: 128 (over y_lo, z, x, core).
Axes of the slice: x: 4, y: 4 (y_hi: 2, y_lo: 2; y = y_hi * 2 + y_lo), z: 8, core: 2. Of those that a mesh axis runs over, the one named last changes fastest.
Arguments:
- feats: bfloat16 [2, 1024, 256, 320], P('branch', 'strip')
- conv_first: bfloat16 [2, 3, 3, 320, 320], P('branch'), may hold values from -0.109375 to 0.109375
- conv_second: bfloat16 [2, 3, 3, 320, 320], P('branch'), may hold values from -0.109375 to 0.109375
- time_shift: float32 [2, 320], P('branch'), may hold values from -6 to 6
- norm_gains: float32 [2, 2, 320], P('branch'), may hold values from 0.1 to 1.9
- zero_conv: bfloat16 [320, 320], replicated, may hold values from -0.3125 to 0.3125
Outputs:
- outputs: bfloat16 [2, 1024, 256, 320], P('branch', 'strip')
The draws below stay inside these ranges and needn't reach their ends.
All inputs are finite; a program needn't handle non-finite values.
Results may differ from the reference program's by a relative error of at most 0.0042.
The reference program's roundings to bfloat16 on the way (of `first`, `second`, `control` and `residual`) count: a program that leaves them out, or rounds other values in their place, can miss the bound.
Values may be sent and summed in bfloat16 or wider, within the bound.
No kernel may reach another device: no remote copies, remote signals or barrier semaphores. Data moves between devices by JAX's collectives and lax.ppermute only.
A program may use at most 64 MiB of HBM per device.

```python
import jax
import jax.numpy as jnp
from jax import lax

C = 320
G = 32
ROWS = 8
W = 256
H = 1024


def draw_feats(key, part):
    key = jax.random.fold_in(key, 5)
    key_base = jax.random.fold_in(key, 0)
    key_rows = jax.random.fold_in(key, 1)
    key_level = jax.random.fold_in(key, 3)
    key_offset = jax.random.fold_in(key, 4)
    blocks = H // ROWS
    ramp = 1.0 + 2.0 * jnp.arange(H, dtype=jnp.float32) / (H - 1)
    rough = jax.random.uniform(key_rows, (2, H), jnp.float32, 0.6, 1.4)
    level = jnp.exp(jax.random.uniform(key_level, (2, blocks), jnp.float32, -1.5, 1.5)) / 1.8
    offset = jax.random.uniform(key_offset, (2, blocks, C), jnp.float32, -1.0, 1.0)
    level_rows = jnp.repeat(level, ROWS, axis=1)
    offset_rows = jnp.repeat(offset, ROWS, axis=1)[:, :, None, :]
    row_scale = (ramp[None, :] * rough * level_rows)[:, :, None, None]
    values = (jax.random.normal(key_base, (2, H, W, C), jnp.float32) + offset_rows) * row_scale
    return values.astype(jnp.bfloat16)


def block_scale(stream_key, extent, pieces, smallest, high):
    def one(axis_at, parts):
        steps = jax.random.uniform(jax.random.fold_in(jax.random.fold_in(stream_key, 6), axis_at), (parts,), jnp.float32, smallest / len(pieces), high / len(pieces))
        return jnp.repeat(jnp.exp(steps), extent[axis_at] // parts).reshape((-1,) + (1,) * (len(extent) - axis_at - 1))

    level = one(*pieces[0])
    for cut in pieces[1:]:
        level = level * one(*cut)
    return level


def normal_values(own_key, dims, spread, most, cuts=(), kind=jnp.bfloat16):
    values = jax.random.normal(own_key, dims, jnp.float32) * spread
    if len(cuts) > 0:
        values = block_scale(own_key, dims, cuts, -0.22, 0.18) * values
    return jnp.clip(values, min=-most, max=most).astype(kind)


def setup_inputs(seed: int = 0) -> dict:
    seeds = jax.random.split(jax.random.key(seed), 7)
    feats = draw_feats(jax.random.fold_in(seeds[6], 71), 0)
    conv_first = normal_values(seeds[1], (2, 3, 3, C, C), (9 * C) ** -0.5, 0.109375, ((0, 2),))
    conv_second = normal_values(seeds[2], (2, 3, 3, C, C), (9 * C) ** -0.5, 0.109375, ((0, 2),))
    time_shift = normal_values(seeds[3], (2, C), 1.0, 6.0, ((0, 2),), jnp.float32)
    norm_gains = jnp.clip(1.0 + 0.18 * jax.random.normal(seeds[4], (2, 2, C), jnp.float32), 0.1, 1.9)
    zero_conv = normal_values(seeds[5], (C, C), C ** -0.5, 0.3125)
    return {"feats": feats, "conv_first": conv_first, "conv_second": conv_second, "time_shift": time_shift, "norm_gains": norm_gains, "zero_conv": zero_conv}


def group_norm(values, gain):
    grouped = values.reshape(values.shape[0], values.shape[1], G, C // G)
    mean = lax.optimization_barrier(jnp.mean(grouped, axis=(0, 1, 3), keepdims=True))
    centered = grouped - mean
    variance = lax.optimization_barrier(jnp.mean(centered * centered, axis=(0, 1, 3), keepdims=True))
    normed = centered / jnp.sqrt(variance + 1e-05)
    return normed.reshape(values.shape) * gain

def conv_same(inputs, kernel):
    result = lax.conv_general_dilated(inputs.astype(jnp.float32)[None], kernel.astype(jnp.float32), (1, 1), ((1, 1), (1, 1)), dimension_numbers=('NHWC', 'HWIO', 'NHWC'))
    return result[0]

def one_copy(feats, conv_first, conv_second, time_shift, norm_gains, index):
    source = feats[index].astype(jnp.float32)
    first = jax.nn.silu(group_norm(source, norm_gains[index, 0])).astype(jnp.bfloat16)
    middle = conv_same(first, conv_first[index]) + time_shift[index]
    second = jax.nn.silu(group_norm(middle, norm_gains[index, 1])).astype(jnp.bfloat16)
    return source + conv_same(second, conv_second[index])

def reference(feats, conv_first, conv_second, time_shift, norm_gains, zero_conv):
    control = one_copy(feats, conv_first, conv_second, time_shift, norm_gains, 0).astype(jnp.bfloat16)
    residual = jnp.dot(control.reshape(-1, C), zero_conv, preferred_element_type=jnp.float32).astype(jnp.bfloat16)
    unet = one_copy(feats, conv_first, conv_second, time_shift, norm_gains, 1)
    mixed = (unet + residual.reshape(unet.shape).astype(jnp.float32)).astype(jnp.bfloat16)
    return jnp.stack([control, mixed])
```

```python
import functools

import jax
import jax.numpy as jnp
from jax import lax
from jax.experimental import pallas as pl
from jax.experimental.pallas import tpu as pltpu
from jax.sharding import PartitionSpec as P

G = 32
F32 = jnp.float32
BF16 = jnp.bfloat16
VMEM = pl.BlockSpec(memory_space=pltpu.VMEM)
SMEM = pl.BlockSpec(memory_space=pltpu.SMEM)
LANES = 128
EARLY = 2


def call(kernel, name, ins, outs, scratch, mib, flops):
    return pl.pallas_call(
        kernel,
        out_shape=outs,
        in_specs=[SMEM] + [VMEM] * ins,
        out_specs=[VMEM] * len(outs),
        scratch_shapes=scratch,
        compiler_params=pltpu.CompilerParams(vmem_limit_bytes=mib * 2**20),
        cost_estimate=pl.CostEstimate(flops=flops, bytes_accessed=4 * 2**20, transcendentals=0),
        name=name,
    )


def group_masks(channels):
    per = channels // G
    ch = lax.broadcasted_iota(jnp.int32, (channels, LANES), 0)
    low = lax.broadcasted_iota(jnp.int32, (channels, LANES), 1) * per
    high = low - G * per
    first = jnp.where((ch >= low) & (ch < low + per), 1.0, 0.0)
    second = jnp.where((ch >= high) & (ch < high + per), 1.0, 0.0)
    return first, second


def column(row):
    n = row.shape[1]
    eye = lax.broadcasted_iota(jnp.int32, (n, n), 0) == lax.broadcasted_iota(jnp.int32, (n, n), 1)
    return jnp.sum(jnp.where(eye, row, 0.0), axis=1, keepdims=True)


def fold(x):
    parts = [x[:, i : i + LANES] for i in range(0, x.shape[1], LANES)]
    return functools.reduce(jnp.add, parts)


def strip_stats(load, rows, channels, width):
    first, second = group_masks(channels)
    count = rows * width * (channels // G)
    total = functools.reduce(jnp.add, [fold(load(r)) for r in range(rows)])
    total = jnp.sum(total, axis=1, keepdims=True)
    mean = jnp.sum(first * total, axis=0, keepdims=True) / count
    mean_c = jnp.sum(first * mean, axis=1, keepdims=True)
    squares = functools.reduce(
        jnp.add, [fold((load(r) - mean_c) * (load(r) - mean_c)) for r in range(rows)]
    )
    squares = jnp.sum(squares, axis=1, keepdims=True)
    return mean + jnp.sum(second * squares, axis=0, keepdims=True)


def whole_stats(stats, channels, count):
    first, second = group_masks(channels)
    strips = stats.shape[0]
    total = jnp.sum(stats, axis=0, keepdims=True)
    mean = total / strips
    off = stats - mean
    between = jnp.sum(off * off, axis=0, keepdims=True) * count
    mean_c = jnp.sum(first * mean, axis=1, keepdims=True)
    variance = jnp.sum(first * between + second * total, axis=1, keepdims=True) / (strips * count)
    return mean_c, lax.rsqrt(variance + 1e-5)


def silu(v):
    half = 0.5 * v
    return half + half * jnp.tanh(half)


def turned(w, out):
    c = w.shape[2]
    for kx in range(3):
        out[kx * c : (kx + 1) * c, :] = jnp.concatenate([w[ky, kx].T for ky in range(3)], axis=1)


def conv_row(wt, rows):
    c, w = rows.shape[0] // 3, rows.shape[1]
    y = jnp.dot(wt, rows, preferred_element_type=F32)
    lane = lax.broadcasted_iota(jnp.int32, (c, w), 1)
    left = jnp.where(lane == 0, 0.0, pltpu.roll(y[:c], 1, 1))
    right = jnp.where(lane == w - 1, 0.0, pltpu.roll(y[2 * c :], w - 1, 1))
    return y[c : 2 * c] + left + right


def stats_kernel(pos, x, w, out, wt):
    rows, c, width = x.shape
    st = strip_stats(lambda r: x[r].astype(F32), rows, c, width)
    out[...] = jnp.broadcast_to(st, out.shape)
    turned(w, wt)


def first_kernel(pos, x, low, high, st, gains, shift, wt, w2, z, mid, out, w2t, zt, acts):
    rows, c, width = x.shape
    mean, scale = whole_stats(st[...], c, rows * width * (c // G))
    scale = scale * column(gains[0:1, :])
    shift_c = column(shift[...])
    top = jnp.where(pos[0] == 0, 0.0, 1.0)
    bottom = jnp.where(pos[0] == pos[1] - 1, 0.0, 1.0)

    def put(at):
        if at < 2:
            v, keep = low[at], top
        elif at < rows + 2:
            v, keep = x[at - 2], None
        else:
            v, keep = high[at - rows - 2], bottom
        a = silu((v.astype(F32) - mean) * scale)
        if keep is not None:
            a = a * keep
        acts[at * c : (at + 1) * c, :] = a.astype(BF16)

    for at in range(3):
        put(at)
    for r in range(rows + 2):
        mid[r] = conv_row(wt[...], acts[r * c : (r + 3) * c, :]) + shift_c
        if r + 3 < rows + 4:
            put(r + 3)
    turned(w2, w2t)
    zt[...] = z[...].T
    st2 = strip_stats(lambda r: mid[r + 1], rows, c, width)
    out[...] = jnp.broadcast_to(st2, out.shape)


def second_kernel(begin, end, pos, x, mid, st, gains, w2t, zt, block, residual, acts):
    rows, c, width = x.shape
    mean, scale = whole_stats(st[...], c, rows * width * (c // G))
    scale = scale * column(gains[1:2, :])
    top = jnp.where(pos[0] == 0, 0.0, 1.0)
    bottom = jnp.where(pos[0] == pos[1] - 1, 0.0, 1.0)

    def put(at):
        a = silu((mid[begin + at] - mean) * scale)
        if begin + at == 0:
            a = a * top
        if begin + at == rows + 1:
            a = a * bottom
        acts[at * c : (at + 1) * c, :] = a.astype(BF16)

    for at in range(3):
        put(at)
    for r in range(end - begin):
        y = x[begin + r].astype(F32) + conv_row(w2t[...], acts[r * c : (r + 3) * c, :])
        block[r] = y
        control = y.astype(BF16)
        residual[r] = jnp.dot(zt[...], control, preferred_element_type=F32).astype(BF16)
        if r + 3 < end - begin + 2:
            put(r + 3)


def mix_kernel(pos, block, arrived, *rest):
    out = rest[-1]
    unet = pos[2] == 1
    for r in range(block.shape[0]):
        add = jnp.where(unet, arrived[r].astype(F32), 0.0)
        out[r] = (block[r] + add).astype(BF16)


def mix(pos, block, arrived, begin, whole, old):
    n, c, width = block.shape
    piece = pl.BlockSpec((EARLY, c, width), lambda i: (i, 0, 0))
    held = [] if old is None else [old]
    return pl.pallas_call(
        mix_kernel,
        out_shape=whole,
        grid=(n // EARLY,),
        in_specs=[SMEM, piece, piece] + [pl.BlockSpec(memory_space=pl.ANY)] * len(held),
        out_specs=pl.BlockSpec((EARLY, c, width), lambda i: (i + begin // EARLY, 0, 0)),
        input_output_aliases={3: 0} if held else {},
        cost_estimate=pl.CostEstimate(flops=10**6, bytes_accessed=2**21, transcendentals=0),
        name="mix",
    )(pos, block, arrived, *held)


def on_device(feats, conv_first, conv_second, time_shift, norm_gains, zero_conv):
    strips = lax.axis_size("strip")
    here = lax.axis_index("strip")
    pos = jnp.stack([here, strips, lax.axis_index("branch")]).astype(jnp.int32)
    x = jnp.transpose(feats[0], (0, 2, 1))
    rows, c, width = x.shape
    down = [(i, i + 1) for i in range(strips - 1)]
    up = [(i + 1, i) for i in range(strips - 1)]
    low = lax.ppermute(x[rows - 2 :], "strip", down)
    high = lax.ppermute(x[:2], "strip", up)
    stat = jax.ShapeDtypeStruct((strips, LANES), F32)
    wide = jax.ShapeDtypeStruct((3 * c, 3 * c), BF16)
    row_macs = 2 * 9 * c * c * width

    def spread(st):
        return lax.all_to_all(st, "strip", 0, 0)

    st1, w1t = call(stats_kernel, "stats_first", 2, (stat, wide), [], 24, 10**7)(
        pos, x, conv_first[0]
    )
    st1 = spread(st1)
    mid, st2, w2t, zt = call(
        first_kernel,
        "conv_first",
        9,
        (
            jax.ShapeDtypeStruct((rows + 2, c, width), F32),
            stat,
            wide,
            jax.ShapeDtypeStruct((c, c), BF16),
        ),
        [pltpu.VMEM(((rows + 4) * c, width), BF16)],
        40,
        10 * row_macs,
    )(pos, x, low, high, st1, norm_gains[0], time_shift, w1t, conv_second[0], zero_conv)
    st2 = spread(st2)
    branches = [(0, 1)]
    pieces = []
    for begin, end in ((0, EARLY), (EARLY, rows)):
        n = end - begin
        block, residual = call(
            functools.partial(second_kernel, begin, end),
            "conv_second",
            6,
            (
                jax.ShapeDtypeStruct((n, c, width), F32),
                jax.ShapeDtypeStruct((n, c, width), BF16),
            ),
            [pltpu.VMEM(((n + 2) * c, width), BF16)],
            32,
            n * row_macs,
        )(pos, x, mid, st2, norm_gains[0], w2t, zt)
        pieces.append((begin, block, lax.ppermute(residual, "branch", branches)))
    whole = jax.ShapeDtypeStruct((rows, c, width), BF16)
    out = None
    for begin, block, arrived in pieces:
        out = mix(pos, block, arrived, begin, whole, out)
    return jnp.transpose(out, (0, 2, 1))[None]


def solution(mesh):
    placed = (
        P("branch", "strip", None, None),
        P("branch", None, None, None, None),
        P("branch", None, None, None, None),
        P("branch", None),
        P("branch", None, None),
        P(),
    )
    return jax.shard_map(
        on_device,
        mesh=mesh,
        in_specs=placed,
        out_specs=P("branch", "strip", None, None),
        check_vma=False,
    )
```

```python
import functools

import jax
import jax.numpy as jnp
from jax import lax
from jax.experimental import pallas as pl
from jax.experimental.pallas import tpu as pltpu
from jax.sharding import PartitionSpec as P

G = 32
F32 = jnp.float32
BF16 = jnp.bfloat16
VMEM = pl.BlockSpec(memory_space=pltpu.VMEM)
SMEM = pl.BlockSpec(memory_space=pltpu.SMEM)
ANYWHERE = pl.BlockSpec(memory_space=pl.ANY)
LANES = 128


def call(kernel, name, ins, outs, scratch, mib, flops, unread=0):
    return pl.pallas_call(
        kernel,
        out_shape=outs,
        in_specs=[SMEM] + [VMEM] * ins + [ANYWHERE] * unread,
        out_specs=[VMEM] * len(outs),
        scratch_shapes=scratch,
        compiler_params=pltpu.CompilerParams(vmem_limit_bytes=mib * 2**20),
        cost_estimate=pl.CostEstimate(flops=flops, bytes_accessed=4 * 2**20, transcendentals=0),
        name=name,
    )


def group_masks(channels):
    per = channels // G
    ch = lax.broadcasted_iota(jnp.int32, (channels, LANES), 0)
    low = lax.broadcasted_iota(jnp.int32, (channels, LANES), 1) * per
    high = low - G * per
    first = jnp.where((ch >= low) & (ch < low + per), 1.0, 0.0)
    second = jnp.where((ch >= high) & (ch < high + per), 1.0, 0.0)
    return first, second


def column(row):
    n = row.shape[1]
    eye = lax.broadcasted_iota(jnp.int32, (n, n), 0) == lax.broadcasted_iota(jnp.int32, (n, n), 1)
    return jnp.sum(jnp.where(eye, row, 0.0), axis=1, keepdims=True)


def fold(x):
    parts = [x[:, i : i + LANES] for i in range(0, x.shape[1], LANES)]
    return functools.reduce(jnp.add, parts)


def strip_stats(load, rows, channels, width):
    first, second = group_masks(channels)
    count = rows * width * (channels // G)
    total = functools.reduce(jnp.add, [fold(load(r)) for r in range(rows)])
    total = jnp.sum(total, axis=1, keepdims=True)
    mean = jnp.sum(first * total, axis=0, keepdims=True) / count
    mean_c = jnp.sum(first * mean, axis=1, keepdims=True)
    squares = functools.reduce(
        jnp.add, [fold((load(r) - mean_c) * (load(r) - mean_c)) for r in range(rows)]
    )
    squares = jnp.sum(squares, axis=1, keepdims=True)
    return mean + jnp.sum(second * squares, axis=0, keepdims=True)


def whole_stats(stats, channels, count):
    first, second = group_masks(channels)
    strips = stats.shape[0]
    total = jnp.sum(stats, axis=0, keepdims=True)
    mean = total / strips
    off = stats - mean
    between = jnp.sum(off * off, axis=0, keepdims=True) * count
    mean_c = jnp.sum(first * mean, axis=1, keepdims=True)
    variance = jnp.sum(first * between + second * total, axis=1, keepdims=True) / (strips * count)
    return mean_c, lax.rsqrt(variance + 1e-5)


def silu(v):
    half = 0.5 * v
    return half + half * jnp.tanh(half)


def turned(w, out):
    c = w.shape[2]
    for kx in range(3):
        out[kx * c : (kx + 1) * c, :] = jnp.concatenate([w[ky, kx].T for ky in range(3)], axis=1)


def conv_row(wt, rows):
    c, w = rows.shape[0] // 3, rows.shape[1]
    y = jnp.dot(wt, rows, preferred_element_type=F32)
    lane = lax.broadcasted_iota(jnp.int32, (c, w), 1)
    left = jnp.where(lane == 0, 0.0, pltpu.roll(y[:c], 1, 1))
    right = jnp.where(lane == w - 1, 0.0, pltpu.roll(y[2 * c :], w - 1, 1))
    return y[c : 2 * c] + left + right


def stats_kernel(pos, x, out, first_rows, last_rows):
    rows, c, width = x.shape
    st = strip_stats(lambda r: x[r].astype(F32), rows, c, width)
    out[...] = jnp.broadcast_to(st, out.shape)
    first_rows[...] = x[:2]
    last_rows[...] = x[rows - 2 :]


def edge_flags(pos):
    return jnp.where(pos[0] == 0, 0.0, 1.0), jnp.where(pos[0] == pos[1] - 1, 0.0, 1.0)


def first_kernel(
    pos, x, low, high, st, gains, shift, w1, w2, z, mid, out, edges, w1t, w2t, zt, cols, acts
):
    rows, c, width = x.shape
    mean, scale = whole_stats(st[...], c, rows * width * (c // G))
    scale = scale * column(gains[0:1, :])
    top, bottom = edge_flags(pos)

    def put(at):
        if at < 2:
            v, keep = low[at], top
        elif at < rows + 2:
            v, keep = x[at - 2], None
        else:
            v, keep = high[at - rows - 2], bottom
        a = silu((v.astype(F32) - mean) * scale)
        if keep is not None:
            a = a * keep
        acts[at * c : (at + 1) * c, :] = a.astype(BF16)

    for at in (1, 2, 3):
        put(at)
    turned(w1, w1t)
    shift_c = column(shift[...])
    cols[...] = jnp.broadcast_to(
        jnp.concatenate([shift_c, column(gains[1:2, :])], axis=0), cols.shape
    )
    first, second = group_masks(c)
    per_row = width * (c // G)
    for r in range(1, rows + 1):
        y = conv_row(w1t[...], acts[r * c : (r + 3) * c, :]) + shift_c
        mid[r - 1] = y
        if r == 1:
            total = fold(y)
            row_sum = jnp.sum(first * jnp.sum(total, axis=1, keepdims=True), axis=0, keepdims=True)
            about = row_sum / per_row
            about_c = jnp.sum(first * about, axis=1, keepdims=True)
            squares = fold((y - about_c) * (y - about_c))
        else:
            total = total + fold(y)
            squares = squares + fold((y - about_c) * (y - about_c))
        if r < rows:
            put(r + 3)
    count = rows * per_row
    total = jnp.sum(total, axis=1, keepdims=True)
    squares = jnp.sum(squares, axis=1, keepdims=True)
    own_mean = jnp.sum(first * total, axis=0, keepdims=True) / count
    off = jnp.sum(first * (own_mean - about), axis=1, keepdims=True)
    squares = squares - off * off * (rows * width)
    st2 = own_mean + jnp.sum(second * squares, axis=0, keepdims=True)
    out[...] = jnp.broadcast_to(st2, out.shape)
    put(0)
    put(rows + 3)
    turned(w2, w2t)
    zt[...] = z[...].T
    edges[: 3 * c, :] = acts[: 3 * c, :]
    edges[3 * c :, :] = acts[(rows + 1) * c :, :]


def second_kernel(wanted, pos, x, mid, st, cols, w2t, zt, edges, w1t, after, *outs):
    block, residual, acts, control = outs
    rows, c, width = x.shape
    mean, scale = whole_stats(st[...], c, rows * width * (c // G))
    scale = scale * cols[c:, :1]
    top, bottom = edge_flags(pos)

    def put(at, slot):
        if at == 0:
            v = conv_row(w1t[...], edges[: 3 * c, :]) + cols[:c, :1]
        elif at == rows + 1:
            v = conv_row(w1t[...], edges[3 * c :, :]) + cols[:c, :1]
        else:
            v = mid[at - 1]
        a = silu((v - mean) * scale)
        if at == 0:
            a = a * top
        if at == rows + 1:
            a = a * bottom
        acts[slot * c : (slot + 1) * c, :] = a.astype(BF16)

    done = 0
    slot = 0
    for begin, end in wanted:
        base = slot
        for at in range(begin, end + 2):
            put(at, slot)
            slot += 1
        for r in range(begin, end):
            at = (base + r - begin) * c
            y = x[r].astype(F32) + conv_row(w2t[...], acts[at : at + 3 * c, :])
            block[done] = y
            control[done * c : (done + 1) * c, :] = y.astype(BF16)
            done += 1
    for r in range(done):
        residual[r] = jnp.dot(
            zt[...], control[r * c : (r + 1) * c, :], preferred_element_type=F32
        ).astype(BF16)


def mix_kernel(wanted, pos, block, arrived, *rest):
    whole, held, sem = rest[-3:]
    unet = pos[2] == 1
    copies = []
    for r, to in enumerate(wanted):
        add = jnp.where(unet, arrived[r].astype(F32), 0.0)
        held[r] = (block[r] + add).astype(BF16)
        copies.append(pltpu.make_async_copy(held.at[r], whole.at[to], sem.at[r]))
        copies[-1].start()
    for copy in copies:
        copy.wait()


def mix(pos, block, arrived, wanted, whole, old):
    held = [] if old is None else [old]
    return pl.pallas_call(
        functools.partial(mix_kernel, wanted),
        out_shape=whole,
        in_specs=[SMEM, VMEM, VMEM] + [ANYWHERE] * len(held),
        out_specs=ANYWHERE,
        scratch_shapes=[
            pltpu.VMEM(arrived.shape, BF16),
            pltpu.SemaphoreType.DMA((len(wanted),)),
        ],
        input_output_aliases={3: 0} if held else {},
        compiler_params=pltpu.CompilerParams(vmem_limit_bytes=16 * 2**20),
        cost_estimate=pl.CostEstimate(flops=10**6, bytes_accessed=2**21, transcendentals=0),
        name="mix",
    )(pos, block, arrived, *held)


def on_device(feats, conv_first, conv_second, time_shift, norm_gains, zero_conv):
    strips = lax.axis_size("strip")
    here = lax.axis_index("strip")
    pos = jnp.stack([here, strips, lax.axis_index("branch")]).astype(jnp.int32)
    x = jnp.transpose(feats[0], (0, 2, 1))
    rows, c, width = x.shape
    down = [(i, i + 1) for i in range(strips - 1)]
    up = [(i + 1, i) for i in range(strips - 1)]
    shaped = jax.ShapeDtypeStruct
    stat = shaped((strips, LANES), F32)
    wide = shaped((3 * c, 3 * c), BF16)
    halo = shaped((2, c, width), BF16)
    row_macs = 2 * 9 * c * c * width

    def spread(st):
        return lax.all_to_all(st, "strip", 0, 0)

    st1, first_rows, last_rows = call(
        stats_kernel, "stats_first", 1, (stat, halo, halo), [], 16, 2 * 10**10
    )(pos, x)
    low = lax.ppermute(last_rows, "strip", down)
    high = lax.ppermute(first_rows, "strip", up)
    st1 = spread(st1)
    mid, st2, edges, w1t, w2t, zt, cols = call(
        first_kernel,
        "conv_first",
        9,
        (
            shaped((rows, c, width), F32),
            stat,
            shaped((6 * c, width), BF16),
            wide,
            wide,
            shaped((c, c), BF16),
            shaped((2 * c, LANES), F32),
        ),
        [pltpu.VMEM(((rows + 4) * c, width), BF16)],
        36,
        rows * row_macs,
    )(pos, x, low, high, st1, norm_gains[0], time_shift, conv_first[0], conv_second[0], zero_conv)
    st2 = spread(st2)
    pieces = []
    after = zt
    for wanted in (((3, 6),), ((0, 3),), ((6, rows),)):
        n = sum(end - begin for begin, end in wanted)
        block, residual = call(
            functools.partial(second_kernel, wanted),
            "conv_second",
            8,
            (shaped((n, c, width), F32), shaped((n, c, width), BF16)),
            [
                pltpu.VMEM(((n + 2 * len(wanted)) * c, width), BF16),
                pltpu.VMEM((n * c, width), BF16),
            ],
            32,
            n * row_macs,
            unread=1,
        )(pos, x, mid, st2, cols, w2t, zt, edges, w1t, after)
        after = residual
        listed = [r for begin, end in wanted for r in range(begin, end)]
        pieces.append((listed, block, lax.ppermute(residual, "branch", [(0, 1)])))
    whole = shaped((rows, c, width), BF16)
    out = None
    for listed, block, arrived in pieces:
        out = mix(pos, block, arrived, listed, whole, out)
    return jnp.transpose(out, (0, 2, 1))[None]


def solution(mesh):
    placed = (
        P("branch", "strip", None, None),
        P("branch", None, None, None, None),
        P("branch", None, None, None, None),
        P("branch", None),
        P("branch", None, None),
        P(),
    )
    return jax.shard_map(
        on_device,
        mesh=mesh,
        in_specs=placed,
        out_specs=P("branch", "strip", None, None),
        check_vma=False,
    )
```

```python
import functools

import jax
import jax.numpy as jnp
from jax import lax
from jax.experimental import pallas as pl
from jax.experimental.pallas import tpu as pltpu
from jax.sharding import PartitionSpec as P

G = 32
F32 = jnp.float32
BF16 = jnp.bfloat16
VMEM = pl.BlockSpec(memory_space=pltpu.VMEM)
ANYWHERE = pl.BlockSpec(memory_space=pl.ANY)
LANES = 128


def call(kernel, name, ins, outs, scratch, mib, flops, unread=0):
    return pl.pallas_call(
        kernel,
        out_shape=outs,
        in_specs=[VMEM] * ins + [ANYWHERE] * unread,
        out_specs=[VMEM] * len(outs),
        scratch_shapes=scratch,
        compiler_params=pltpu.CompilerParams(vmem_limit_bytes=mib * 2**20),
        cost_estimate=pl.CostEstimate(flops=flops, bytes_accessed=4 * 2**20, transcendentals=0),
        name=name,
    )


def group_masks(channels):
    per = channels // G
    ch = lax.broadcasted_iota(jnp.int32, (channels, LANES), 0)
    low = lax.broadcasted_iota(jnp.int32, (channels, LANES), 1) * per
    high = low - G * per
    first = jnp.where((ch >= low) & (ch < low + per), 1.0, 0.0)
    second = jnp.where((ch >= high) & (ch < high + per), 1.0, 0.0)
    return first, second


def column(row):
    n = row.shape[1]
    eye = lax.broadcasted_iota(jnp.int32, (n, n), 0) == lax.broadcasted_iota(jnp.int32, (n, n), 1)
    return jnp.sum(jnp.where(eye, row, 0.0), axis=1, keepdims=True)


def fold(x):
    parts = [x[:, i : i + LANES] for i in range(0, x.shape[1], LANES)]
    return functools.reduce(jnp.add, parts)


def strip_stats(load, rows, channels, width):
    first, second = group_masks(channels)
    count = rows * width * (channels // G)
    total = functools.reduce(jnp.add, [fold(load(r)) for r in range(rows)])
    total = jnp.sum(total, axis=1, keepdims=True)
    mean = jnp.sum(first * total, axis=0, keepdims=True) / count
    mean_c = jnp.sum(first * mean, axis=1, keepdims=True)
    squares = functools.reduce(
        jnp.add, [fold((load(r) - mean_c) * (load(r) - mean_c)) for r in range(rows)]
    )
    squares = jnp.sum(squares, axis=1, keepdims=True)
    return mean + jnp.sum(second * squares, axis=0, keepdims=True)


def whole_stats(stats, channels, count):
    first, second = group_masks(channels)
    strips = stats.shape[0]
    total = jnp.sum(stats, axis=0, keepdims=True)
    mean = total / strips
    off = stats - mean
    between = jnp.sum(off * off, axis=0, keepdims=True) * count
    mean_c = jnp.sum(first * mean, axis=1, keepdims=True)
    variance = jnp.sum(first * between + second * total, axis=1, keepdims=True) / (strips * count)
    return mean_c, lax.rsqrt(variance + 1e-5)


def silu(v):
    half = 0.5 * v
    return half + half * jnp.tanh(half)


def turned(w, out):
    c = w.shape[2]
    for kx in range(3):
        out[kx * c : (kx + 1) * c, :] = jnp.concatenate([w[ky, kx].T for ky in range(3)], axis=1)


def conv_row(wt, rows):
    c, w = rows.shape[0] // 3, rows.shape[1]
    y = jnp.dot(wt, rows, preferred_element_type=F32)
    lane = lax.broadcasted_iota(jnp.int32, (c, w), 1)
    left = jnp.where(lane == 0, 0.0, pltpu.roll(y[:c], 1, 1))
    right = jnp.where(lane == w - 1, 0.0, pltpu.roll(y[2 * c :], w - 1, 1))
    return y[c : 2 * c] + left + right


def stats_kernel(flags, x, out, inner, outer):
    rows, c, width = x.shape
    st = strip_stats(lambda r: x[r].astype(F32), rows, c, width)
    out[...] = jnp.broadcast_to(st, out.shape)
    even = flags[3:4, :1] > 0.5
    for i in range(2):
        begin, end = x[i].astype(F32), x[rows - 2 + i].astype(F32)
        inner[i] = jnp.where(even, end, begin).astype(BF16)
        outer[i] = jnp.where(even, begin, end).astype(BF16)


def strip_flags(strips):
    here = lax.axis_index("strip")
    values = [here > 0, here < strips - 1, lax.axis_index("branch") == 1, here % 2 == 0]
    at = lax.broadcasted_iota(jnp.int32, (8, LANES), 0)
    return functools.reduce(
        jnp.add, [jnp.where((at == i) & v, 1.0, 0.0) for i, v in enumerate(values)]
    )


def first_kernel(
    flags, x, inner, outer, st, gains, shift, w1, w2, z, mid, out, edges, w1t, w2t, zt, cols, acts
):
    rows, c, width = x.shape
    mean, scale = whole_stats(st[...], c, rows * width * (c // G))
    scale = scale * column(gains[0:1, :])
    top, bottom = flags[0:1, :1], flags[1:2, :1]
    even = flags[3:4, :1] > 0.5

    def put(at):
        if at < 2:
            v, keep = jnp.where(even, outer[at].astype(F32), inner[at].astype(F32)), top
        elif at < rows + 2:
            v, keep = x[at - 2].astype(F32), None
        else:
            at_high = at - rows - 2
            v = jnp.where(even, inner[at_high].astype(F32), outer[at_high].astype(F32))
            keep = bottom
        a = silu((v - mean) * scale)
        if keep is not None:
            a = a * keep
        acts[at * c : (at + 1) * c, :] = a.astype(BF16)

    for at in (1, 2, 3):
        put(at)
    turned(w1, w1t)
    shift_c = column(shift[...])
    cols[...] = jnp.broadcast_to(
        jnp.concatenate([shift_c, column(gains[1:2, :])], axis=0), cols.shape
    )
    first, second = group_masks(c)
    per_row = width * (c // G)
    for r in range(1, rows + 1):
        y = conv_row(w1t[...], acts[r * c : (r + 3) * c, :]) + shift_c
        mid[r - 1] = y
        if r == 1:
            total = fold(y)
            row_sum = jnp.sum(first * jnp.sum(total, axis=1, keepdims=True), axis=0, keepdims=True)
            about = row_sum / per_row
            about_c = jnp.sum(first * about, axis=1, keepdims=True)
            squares = fold((y - about_c) * (y - about_c))
        else:
            total = total + fold(y)
            squares = squares + fold((y - about_c) * (y - about_c))
        if r < rows:
            put(r + 3)
    count = rows * per_row
    total = jnp.sum(total, axis=1, keepdims=True)
    squares = jnp.sum(squares, axis=1, keepdims=True)
    own_mean = jnp.sum(first * total, axis=0, keepdims=True) / count
    off = jnp.sum(first * (own_mean - about), axis=1, keepdims=True)
    squares = squares - off * off * (rows * width)
    st2 = own_mean + jnp.sum(second * squares, axis=0, keepdims=True)
    out[...] = jnp.broadcast_to(st2, out.shape)
    put(0)
    put(rows + 3)
    turned(w2, w2t)
    zt[...] = z[...].T
    edges[: 3 * c, :] = acts[: 3 * c, :]
    edges[3 * c :, :] = acts[(rows + 1) * c :, :]


def second_kernel(wanted, flags, x, mid, st, cols, w2t, zt, edges, w1t, after, *outs):
    block, residual, acts, control = outs
    rows, c, width = x.shape
    mean, scale = whole_stats(st[...], c, rows * width * (c // G))
    scale = scale * cols[c:, :1]
    top, bottom = flags[0:1, :1], flags[1:2, :1]

    def put(at, slot):
        if at == 0:
            v = conv_row(w1t[...], edges[: 3 * c, :]) + cols[:c, :1]
        elif at == rows + 1:
            v = conv_row(w1t[...], edges[3 * c :, :]) + cols[:c, :1]
        else:
            v = mid[at - 1]
        a = silu((v - mean) * scale)
        if at == 0:
            a = a * top
        if at == rows + 1:
            a = a * bottom
        acts[slot * c : (slot + 1) * c, :] = a.astype(BF16)

    done = 0
    slot = 0
    for begin, end in wanted:
        base = slot
        for at in range(begin, end + 2):
            put(at, slot)
            slot += 1
        for r in range(begin, end):
            at = (base + r - begin) * c
            y = x[r].astype(F32) + conv_row(w2t[...], acts[at : at + 3 * c, :])
            block[done] = y
            control[done * c : (done + 1) * c, :] = y.astype(BF16)
            done += 1
    for r in range(done):
        residual[r] = jnp.dot(
            zt[...], control[r * c : (r + 1) * c, :], preferred_element_type=F32
        ).astype(BF16)


def mix_kernel(wanted, flags, block, arrived, *rest):
    whole, held, sem = rest[-3:]
    unet = flags[2:3, :1] > 0.5
    copies = []
    for r, to in enumerate(wanted):
        add = jnp.where(unet, arrived[r].astype(F32), 0.0)
        held[r] = (block[r] + add).astype(BF16)
        copies.append(pltpu.make_async_copy(held.at[r], whole.at[to], sem.at[r]))
        copies[-1].start()
    for copy in copies:
        copy.wait()


def mix(flags, block, arrived, wanted, whole, old):
    held = [] if old is None else [old]
    return pl.pallas_call(
        functools.partial(mix_kernel, wanted),
        out_shape=whole,
        in_specs=[VMEM, VMEM, VMEM] + [ANYWHERE] * len(held),
        out_specs=ANYWHERE,
        scratch_shapes=[
            pltpu.VMEM(arrived.shape, BF16),
            pltpu.SemaphoreType.DMA((len(wanted),)),
        ],
        input_output_aliases={3: 0} if held else {},
        compiler_params=pltpu.CompilerParams(vmem_limit_bytes=16 * 2**20),
        cost_estimate=pl.CostEstimate(flops=10**6, bytes_accessed=2**21, transcendentals=0),
        name="mix",
    )(flags, block, arrived, *held)


def on_device(feats, conv_first, conv_second, time_shift, norm_gains, zero_conv):
    strips = lax.axis_size("strip")
    flags = strip_flags(strips)
    x = jnp.transpose(feats[0], (0, 2, 1))
    rows, c, width = x.shape
    same_chip = [(i, i ^ 1) for i in range(strips)]
    next_chip = [(i, i + 1) for i in range(1, strips - 1, 2)]
    next_chip += [(target, source) for source, target in next_chip]
    shaped = jax.ShapeDtypeStruct
    stat = shaped((strips, LANES), F32)
    wide = shaped((3 * c, 3 * c), BF16)
    halo = shaped((2, c, width), BF16)
    row_macs = 2 * 9 * c * c * width

    def spread(st):
        return lax.all_to_all(st, "strip", 0, 0)

    st1, inner, outer = call(
        stats_kernel, "stats_first", 2, (stat, halo, halo), [], 16, 2 * 10**10
    )(flags, x)
    outer = lax.ppermute(outer, "strip", next_chip)
    inner = lax.ppermute(inner, "strip", same_chip)
    st1 = spread(st1)
    mid, st2, edges, w1t, w2t, zt, cols = call(
        first_kernel,
        "conv_first",
        10,
        (
            shaped((rows, c, width), F32),
            stat,
            shaped((6 * c, width), BF16),
            wide,
            wide,
            shaped((c, c), BF16),
            shaped((2 * c, LANES), F32),
        ),
        [pltpu.VMEM(((rows + 4) * c, width), BF16)],
        36,
        rows * row_macs,
    )(flags, x, inner, outer, st1, norm_gains[0], time_shift, conv_first[0], conv_second[0], zero_conv)
    st2 = spread(st2)
    pieces = []
    after = zt
    for wanted in (((3, 5),), ((1, 3),), ((5, 7),), ((0, 1), (7, rows))):
        n = sum(end - begin for begin, end in wanted)
        block, residual = call(
            functools.partial(second_kernel, wanted),
            "conv_second",
            9,
            (shaped((n, c, width), F32), shaped((n, c, width), BF16)),
            [
                pltpu.VMEM(((n + 2 * len(wanted)) * c, width), BF16),
                pltpu.VMEM((n * c, width), BF16),
            ],
            32,
            n * row_macs,
            unread=1,
        )(flags, x, mid, st2, cols, w2t, zt, edges, w1t, after)
        after = residual
        listed = [r for begin, end in wanted for r in range(begin, end)]
        pieces.append((listed, block, lax.ppermute(residual, "branch", [(0, 1)])))
    whole = shaped((rows, c, width), BF16)
    out = None
    for listed, block, arrived in pieces:
        out = mix(flags, block, arrived, listed, whole, out)
    return jnp.transpose(out, (0, 2, 1))[None]


def solution(mesh):
    placed = (
        P("branch", "strip", None, None),
        P("branch", None, None, None, None),
        P("branch", None, None, None, None),
        P("branch", None),
        P("branch", None, None),
        P(),
    )
    return jax.shard_map(
        on_device,
        mesh=mesh,
        in_specs=placed,
        out_specs=P("branch", "strip", None, None),
        check_vma=False,
    )
```

```python
import functools

import jax
import jax.numpy as jnp
from jax import lax
from jax.experimental import pallas as pl
from jax.experimental.pallas import tpu as pltpu
from jax.sharding import PartitionSpec as P

G = 32
F32 = jnp.float32
BF16 = jnp.bfloat16
VMEM = pl.BlockSpec(memory_space=pltpu.VMEM)
ANYWHERE = pl.BlockSpec(memory_space=pl.ANY)
LANES = 128


def call(kernel, name, ins, outs, scratch, mib, flops, unread=0):
    return pl.pallas_call(
        kernel,
        out_shape=outs,
        in_specs=[VMEM] * ins + [ANYWHERE] * unread,
        out_specs=[VMEM] * len(outs),
        scratch_shapes=scratch,
        compiler_params=pltpu.CompilerParams(vmem_limit_bytes=mib * 2**20),
        cost_estimate=pl.CostEstimate(flops=flops, bytes_accessed=4 * 2**20, transcendentals=0),
        name=name,
    )


def group_masks(channels):
    per = channels // G
    ch = lax.broadcasted_iota(jnp.int32, (channels, LANES), 0)
    low = lax.broadcasted_iota(jnp.int32, (channels, LANES), 1) * per
    high = low - G * per
    first = jnp.where((ch >= low) & (ch < low + per), 1.0, 0.0)
    second = jnp.where((ch >= high) & (ch < high + per), 1.0, 0.0)
    return first, second


def column(row):
    n = row.shape[1]
    eye = lax.broadcasted_iota(jnp.int32, (n, n), 0) == lax.broadcasted_iota(jnp.int32, (n, n), 1)
    return jnp.sum(jnp.where(eye, row, 0.0), axis=1, keepdims=True)


def fold(x):
    parts = [x[:, i : i + LANES] for i in range(0, x.shape[1], LANES)]
    return functools.reduce(jnp.add, parts)


def strip_stats(load, rows, channels, width):
    first, second = group_masks(channels)
    count = rows * width * (channels // G)
    total = functools.reduce(jnp.add, [fold(load(r)) for r in range(rows)])
    total = jnp.sum(total, axis=1, keepdims=True)
    mean = jnp.sum(first * total, axis=0, keepdims=True) / count
    mean_c = jnp.sum(first * mean, axis=1, keepdims=True)
    squares = functools.reduce(
        jnp.add, [fold((load(r) - mean_c) * (load(r) - mean_c)) for r in range(rows)]
    )
    squares = jnp.sum(squares, axis=1, keepdims=True)
    return mean + jnp.sum(second * squares, axis=0, keepdims=True)


def whole_stats(stats, channels, count):
    first, second = group_masks(channels)
    strips = stats.shape[0]
    total = jnp.sum(stats, axis=0, keepdims=True)
    mean = total / strips
    off = stats - mean
    between = jnp.sum(off * off, axis=0, keepdims=True) * count
    mean_c = jnp.sum(first * mean, axis=1, keepdims=True)
    variance = jnp.sum(first * between + second * total, axis=1, keepdims=True) / (strips * count)
    return mean_c, lax.rsqrt(variance + 1e-5)


def silu(v):
    half = 0.5 * v
    return half + half * jnp.tanh(half)


def turned(w, out, kx):
    c = w.shape[2]
    out[kx * c : (kx + 1) * c, :] = jnp.concatenate([w[ky, kx].T for ky in range(3)], axis=1)


def conv_row(wt, rows):
    c, w = rows.shape[0] // 3, rows.shape[1]
    y = jnp.dot(wt, rows, preferred_element_type=F32)
    lane = lax.broadcasted_iota(jnp.int32, (c, w), 1)
    left = jnp.where(lane == 0, 0.0, pltpu.roll(y[:c], 1, 1))
    right = jnp.where(lane == w - 1, 0.0, pltpu.roll(y[2 * c :], w - 1, 1))
    return y[c : 2 * c] + left + right


def stats_kernel(flags, x, out, inner, outer):
    rows, c, width = x.shape
    st = strip_stats(lambda r: x[r].astype(F32), rows, c, width)
    out[...] = jnp.broadcast_to(st, out.shape)
    even = flags[3:4, :1] > 0.5
    for i in range(2):
        begin, end = x[i].astype(F32), x[rows - 2 + i].astype(F32)
        inner[i] = jnp.where(even, end, begin).astype(BF16)
        outer[i] = jnp.where(even, begin, end).astype(BF16)


def strip_flags(strips):
    here = lax.axis_index("strip")
    values = [here > 0, here < strips - 1, lax.axis_index("branch") == 1, here % 2 == 0]
    at = lax.broadcasted_iota(jnp.int32, (8, LANES), 0)
    return functools.reduce(
        jnp.add, [jnp.where((at == i) & v, 1.0, 0.0) for i, v in enumerate(values)]
    )


def first_kernel(
    flags, x, inner, outer, st, gains, shift, w1, w2, z, mid, out, edges, w1t, w2t, zt, cols, acts
):
    rows, c, width = x.shape
    mean, scale = whole_stats(st[...], c, rows * width * (c // G))
    scale = scale * column(gains[0:1, :])
    top, bottom = flags[0:1, :1], flags[1:2, :1]
    even = flags[3:4, :1] > 0.5

    def put(at):
        if at < 2:
            v, keep = jnp.where(even, outer[at].astype(F32), inner[at].astype(F32)), top
        elif at < rows + 2:
            v, keep = x[at - 2].astype(F32), None
        else:
            at_high = at - rows - 2
            v = jnp.where(even, inner[at_high].astype(F32), outer[at_high].astype(F32))
            keep = bottom
        a = silu((v - mean) * scale)
        if keep is not None:
            a = a * keep
        a = a.astype(BF16)
        acts[at * c : (at + 1) * c, :] = a
        if at < 3:
            edges[at * c : (at + 1) * c, :] = a
        if at > rows:
            edges[(at - rows + 2) * c : (at - rows + 3) * c, :] = a

    for kx in range(3):
        turned(w1, w1t, kx)
    for at in (1, 2, 3):
        put(at)
    shift_c = column(shift[...])
    first, second = group_masks(c)
    per_row = width * (c // G)

    def turn_z():
        zt[...] = z[...].T

    def keep_columns():
        both = jnp.concatenate([shift_c, column(gains[1:2, :])], axis=0)
        cols[...] = jnp.broadcast_to(both, cols.shape)

    beside = {
        1: keep_columns,
        2: lambda: turned(w2, w2t, 0),
        3: lambda: turned(w2, w2t, 1),
        4: lambda: turned(w2, w2t, 2),
        5: turn_z,
        6: lambda: put(0),
        7: lambda: put(rows + 3),
    }
    for r in range(1, rows + 1):
        y = conv_row(w1t[...], acts[r * c : (r + 3) * c, :]) + shift_c
        mid[r - 1] = y
        if r == 1:
            total = fold(y)
            row_sum = jnp.sum(first * jnp.sum(total, axis=1, keepdims=True), axis=0, keepdims=True)
            about = row_sum / per_row
            about_c = jnp.sum(first * about, axis=1, keepdims=True)
            squares = fold((y - about_c) * (y - about_c))
        else:
            total = total + fold(y)
            squares = squares + fold((y - about_c) * (y - about_c))
        if r < rows:
            put(r + 3)
        if r in beside:
            beside[r]()
    count = rows * per_row
    total = jnp.sum(total, axis=1, keepdims=True)
    squares = jnp.sum(squares, axis=1, keepdims=True)
    own_mean = jnp.sum(first * total, axis=0, keepdims=True) / count
    moved = (own_mean - about) * (own_mean - about) * count
    moved = pltpu.roll(jnp.broadcast_to(moved, (8, LANES)), G, 1)[:1]
    st2 = own_mean + jnp.sum(second * squares, axis=0, keepdims=True) - moved
    out[...] = jnp.broadcast_to(st2, out.shape)


def second_kernel(wanted, flags, x, mid, st, cols, w2t, zt, edges, w1t, after, *outs):
    block, residual, acts, control = outs
    rows, c, width = x.shape
    mean, scale = whole_stats(st[...], c, rows * width * (c // G))
    scale = scale * cols[c:, :1]
    top, bottom = flags[0:1, :1], flags[1:2, :1]

    def put(at, slot):
        if at == 0:
            v = conv_row(w1t[...], edges[: 3 * c, :]) + cols[:c, :1]
        elif at == rows + 1:
            v = conv_row(w1t[...], edges[3 * c :, :]) + cols[:c, :1]
        else:
            v = mid[at - 1]
        a = silu((v - mean) * scale)
        if at == 0:
            a = a * top
        if at == rows + 1:
            a = a * bottom
        acts[slot * c : (slot + 1) * c, :] = a.astype(BF16)

    done = 0
    slot = 0
    for begin, end in wanted:
        base = slot
        for at in range(begin, end + 2):
            put(at, slot)
            slot += 1
        for r in range(begin, end):
            at = (base + r - begin) * c
            y = x[r].astype(F32) + conv_row(w2t[...], acts[at : at + 3 * c, :])
            block[done] = y
            control[done * c : (done + 1) * c, :] = y.astype(BF16)
            done += 1
    for r in range(done):
        residual[r] = jnp.dot(
            zt[...], control[r * c : (r + 1) * c, :], preferred_element_type=F32
        ).astype(BF16)


def mix_kernel(wanted, flags, block, arrived, *rest):
    whole, held, sem = rest[-3:]
    unet = flags[2:3, :1] > 0.5
    copies = []
    for r, to in enumerate(wanted):
        add = jnp.where(unet, arrived[r].astype(F32), 0.0)
        held[r] = (block[r] + add).astype(BF16)
        copies.append(pltpu.make_async_copy(held.at[r], whole.at[to], sem.at[r]))
        copies[-1].start()
    for copy in copies:
        copy.wait()


def mix(flags, block, arrived, wanted, whole, old):
    held = [] if old is None else [old]
    return pl.pallas_call(
        functools.partial(mix_kernel, wanted),
        out_shape=whole,
        in_specs=[VMEM, VMEM, VMEM] + [ANYWHERE] * len(held),
        out_specs=ANYWHERE,
        scratch_shapes=[
            pltpu.VMEM(arrived.shape, BF16),
            pltpu.SemaphoreType.DMA((len(wanted),)),
        ],
        input_output_aliases={3: 0} if held else {},
        compiler_params=pltpu.CompilerParams(vmem_limit_bytes=16 * 2**20),
        cost_estimate=pl.CostEstimate(flops=10**6, bytes_accessed=2**21, transcendentals=0),
        name="mix",
    )(flags, block, arrived, *held)


def on_device(feats, conv_first, conv_second, time_shift, norm_gains, zero_conv):
    strips = lax.axis_size("strip")
    flags = strip_flags(strips)
    x = jnp.transpose(feats[0], (0, 2, 1))
    rows, c, width = x.shape
    same_chip = [(i, i ^ 1) for i in range(strips)]
    next_chip = [(i, i + 1) for i in range(1, strips - 1, 2)]
    next_chip += [(target, source) for source, target in next_chip]
    shaped = jax.ShapeDtypeStruct
    stat = shaped((strips, LANES), F32)
    wide = shaped((3 * c, 3 * c), BF16)
    halo = shaped((2, c, width), BF16)
    row_macs = 2 * 9 * c * c * width

    def spread(st):
        return lax.all_to_all(st, "strip", 0, 0)

    st1, inner, outer = call(
        stats_kernel, "stats_first", 2, (stat, halo, halo), [], 16, 2 * 10**10
    )(flags, x)
    outer = lax.ppermute(outer, "strip", next_chip)
    inner = lax.ppermute(inner, "strip", same_chip)
    st1 = spread(st1)
    mid, st2, edges, w1t, w2t, zt, cols = call(
        first_kernel,
        "conv_first",
        10,
        (
            shaped((rows, c, width), F32),
            stat,
            shaped((6 * c, width), BF16),
            wide,
            wide,
            shaped((c, c), BF16),
            shaped((2 * c, LANES), F32),
        ),
        [pltpu.VMEM(((rows + 4) * c, width), BF16)],
        36,
        rows * row_macs,
    )(flags, x, inner, outer, st1, norm_gains[0], time_shift, conv_first[0], conv_second[0], zero_conv)
    st2 = spread(st2)
    pieces = []
    after = zt
    for wanted in (((3, 5),), ((1, 3),), ((5, 7),), ((0, 1), (7, rows))):
        n = sum(end - begin for begin, end in wanted)
        block, residual = call(
            functools.partial(second_kernel, wanted),
            "conv_second",
            9,
            (shaped((n, c, width), F32), shaped((n, c, width), BF16)),
            [
                pltpu.VMEM(((n + 2 * len(wanted)) * c, width), BF16),
                pltpu.VMEM((n * c, width), BF16),
            ],
            32,
            n * row_macs,
            unread=1,
        )(flags, x, mid, st2, cols, w2t, zt, edges, w1t, after)
        after = residual
        listed = [r for begin, end in wanted for r in range(begin, end)]
        pieces.append((listed, block, lax.ppermute(residual, "branch", [(0, 1), (1, 0)])))
    whole = shaped((rows, c, width), BF16)
    out = None
    for listed, block, arrived in pieces:
        out = mix(flags, block, arrived, listed, whole, out)
    return jnp.transpose(out, (0, 2, 1))[None]


def solution(mesh):
    placed = (
        P("branch", "strip", None, None),
        P("branch", None, None, None, None),
        P("branch", None, None, None, None),
        P("branch", None),
        P("branch", None, None),
        P(),
    )
    return jax.shard_map(
        on_device,
        mesh=mesh,
        in_specs=placed,
        out_specs=P("branch", "strip", None, None),
        check_vma=False,
    )
```

```python
import functools

import jax
import jax.numpy as jnp
from jax import lax
from jax.experimental import pallas as pl
from jax.experimental.pallas import tpu as pltpu
from jax.sharding import PartitionSpec as P

G = 32
F32 = jnp.float32
BF16 = jnp.bfloat16
VMEM = pl.BlockSpec(memory_space=pltpu.VMEM)
ANYWHERE = pl.BlockSpec(memory_space=pl.ANY)
LANES = 128


def call(kernel, name, ins, outs, scratch, mib, flops, unread=0):
    return pl.pallas_call(
        kernel,
        out_shape=outs,
        in_specs=[VMEM] * ins + [ANYWHERE] * unread,
        out_specs=[VMEM] * len(outs),
        scratch_shapes=scratch,
        compiler_params=pltpu.CompilerParams(vmem_limit_bytes=mib * 2**20),
        cost_estimate=pl.CostEstimate(flops=flops, bytes_accessed=4 * 2**20, transcendentals=0),
        name=name,
    )


def group_masks(channels):
    per = channels // G
    ch = lax.broadcasted_iota(jnp.int32, (channels, LANES), 0)
    low = lax.broadcasted_iota(jnp.int32, (channels, LANES), 1) * per
    high = low - G * per
    first = jnp.where((ch >= low) & (ch < low + per), 1.0, 0.0)
    second = jnp.where((ch >= high) & (ch < high + per), 1.0, 0.0)
    return first, second


def column(row):
    n = row.shape[1]
    eye = lax.broadcasted_iota(jnp.int32, (n, n), 0) == lax.broadcasted_iota(jnp.int32, (n, n), 1)
    return jnp.sum(jnp.where(eye, row, 0.0), axis=1, keepdims=True)


def fold(x):
    parts = [x[:, i : i + LANES] for i in range(0, x.shape[1], LANES)]
    return functools.reduce(jnp.add, parts)


def strip_stats(load, rows, channels, width):
    first, second = group_masks(channels)
    count = rows * width * (channels // G)
    total = functools.reduce(jnp.add, [fold(load(r)) for r in range(rows)])
    total = jnp.sum(total, axis=1, keepdims=True)
    mean = jnp.sum(first * total, axis=0, keepdims=True) / count
    mean_c = jnp.sum(first * mean, axis=1, keepdims=True)
    squares = functools.reduce(
        jnp.add, [fold((load(r) - mean_c) * (load(r) - mean_c)) for r in range(rows)]
    )
    squares = jnp.sum(squares, axis=1, keepdims=True)
    return mean + jnp.sum(second * squares, axis=0, keepdims=True)


def whole_stats(stats, channels, count):
    first, second = group_masks(channels)
    strips = stats.shape[0]
    total = jnp.sum(stats, axis=0, keepdims=True)
    mean = total / strips
    off = stats - mean
    between = jnp.sum(off * off, axis=0, keepdims=True) * count
    mean_c = jnp.sum(first * mean, axis=1, keepdims=True)
    variance = jnp.sum(first * between + second * total, axis=1, keepdims=True) / (strips * count)
    return mean_c, lax.rsqrt(variance + 1e-5)


def silu_of_twice(half):
    return half + half * jnp.tanh(half)


def turned(w, out, kx):
    c = w.shape[2]
    out[kx * c : (kx + 1) * c, :] = jnp.concatenate([w[ky, kx].T for ky in range(3)], axis=1)


def conv_row(wt, rows):
    c, w = rows.shape[0] // 3, rows.shape[1]
    y = jnp.dot(wt, rows, preferred_element_type=F32)
    lane = lax.broadcasted_iota(jnp.int32, (c, w), 1)
    left = jnp.where(lane == 0, 0.0, pltpu.roll(y[:c], 1, 1))
    right = jnp.where(lane == w - 1, 0.0, pltpu.roll(y[2 * c :], w - 1, 1))
    return y[c : 2 * c] + left + right


def stats_kernel(flags, x, out, inner, outer):
    rows, c, width = x.shape
    st = strip_stats(lambda r: x[r].astype(F32), rows, c, width)
    out[...] = jnp.broadcast_to(st, out.shape)
    even = flags[3:4, :1] > 0.5
    for i in range(2):
        begin, end = x[i].astype(F32), x[rows - 2 + i].astype(F32)
        inner[i] = jnp.where(even, end, begin).astype(BF16)
        outer[i] = jnp.where(even, begin, end).astype(BF16)


def strip_flags(strips):
    here = lax.axis_index("strip")
    values = [here > 0, here < strips - 1, lax.axis_index("branch") == 1, here % 2 == 0]
    at = lax.broadcasted_iota(jnp.int32, (8, LANES), 0)
    return functools.reduce(
        jnp.add, [jnp.where((at == i) & v, 1.0, 0.0) for i, v in enumerate(values)]
    )


def first_kernel(
    flags, x, inner, outer, st, gains, shift, w1, w2, z, mid, out, edges, w1t, w2t, zt, cols, acts
):
    rows, c, width = x.shape
    mean, scale = whole_stats(st[...], c, rows * width * (c // G))
    scale = 0.5 * scale * column(gains[0:1, :])
    top, bottom = flags[0:1, :1], flags[1:2, :1]
    even = flags[3:4, :1] > 0.5

    def put(at):
        if at < 2:
            v, keep = jnp.where(even, outer[at].astype(F32), inner[at].astype(F32)), top
        elif at < rows + 2:
            v, keep = x[at - 2].astype(F32), None
        else:
            at_high = at - rows - 2
            v = jnp.where(even, inner[at_high].astype(F32), outer[at_high].astype(F32))
            keep = bottom
        a = silu_of_twice((v - mean) * scale)
        if keep is not None:
            a = a * keep
        a = a.astype(BF16)
        acts[at * c : (at + 1) * c, :] = a
        if at < 3:
            edges[at * c : (at + 1) * c, :] = a
        if at > rows:
            edges[(at - rows + 2) * c : (at - rows + 3) * c, :] = a

    for kx in range(3):
        turned(w1, w1t, kx)
    for at in (1, 2, 3):
        put(at)
    shift_c = column(shift[...])
    first, second = group_masks(c)
    per_row = width * (c // G)

    def turn_z():
        zt[...] = z[...].T

    def keep_columns():
        both = jnp.concatenate([shift_c, column(gains[1:2, :])], axis=0)
        cols[...] = jnp.broadcast_to(both, cols.shape)

    beside = {
        1: keep_columns,
        2: lambda: turned(w2, w2t, 0),
        3: lambda: turned(w2, w2t, 1),
        4: lambda: turned(w2, w2t, 2),
        5: turn_z,
        6: lambda: put(0),
        7: lambda: put(rows + 3),
    }
    for r in range(1, rows + 1):
        y = conv_row(w1t[...], acts[r * c : (r + 3) * c, :]) + shift_c
        mid[r - 1] = y
        if r == 1:
            total = fold(y)
            row_sum = jnp.sum(first * jnp.sum(total, axis=1, keepdims=True), axis=0, keepdims=True)
            about = row_sum / per_row
            about_c = jnp.sum(first * about, axis=1, keepdims=True)
            squares = fold((y - about_c) * (y - about_c))
        else:
            total = total + fold(y)
            squares = squares + fold((y - about_c) * (y - about_c))
        if r < rows:
            put(r + 3)
        if r in beside:
            beside[r]()
    count = rows * per_row
    total = jnp.sum(total, axis=1, keepdims=True)
    squares = jnp.sum(squares, axis=1, keepdims=True)
    own_mean = jnp.sum(first * total, axis=0, keepdims=True) / count
    moved = (own_mean - about) * (own_mean - about) * count
    moved = pltpu.roll(jnp.broadcast_to(moved, (8, LANES)), G, 1)[:1]
    st2 = own_mean + jnp.sum(second * squares, axis=0, keepdims=True) - moved
    out[...] = jnp.broadcast_to(st2, out.shape)


def second_kernel(wanted, flags, x, mid, st, cols, w2t, zt, edges, w1t, after, *outs):
    block, residual, acts, control = outs
    rows, c, width = x.shape
    mean, scale = whole_stats(st[...], c, rows * width * (c // G))
    scale = 0.5 * scale * cols[c:, :1]
    top, bottom = flags[0:1, :1], flags[1:2, :1]

    def put(at, slot):
        if at == 0:
            v = conv_row(w1t[...], edges[: 3 * c, :]) + cols[:c, :1]
        elif at == rows + 1:
            v = conv_row(w1t[...], edges[3 * c :, :]) + cols[:c, :1]
        else:
            v = mid[at - 1]
        a = silu_of_twice((v - mean) * scale)
        if at == 0:
            a = a * top
        if at == rows + 1:
            a = a * bottom
        acts[slot * c : (slot + 1) * c, :] = a.astype(BF16)

    done = 0
    slot = 0
    for begin, end in wanted:
        base = slot
        for at in range(begin, end + 2):
            put(at, slot)
            slot += 1
        for r in range(begin, end):
            at = (base + r - begin) * c
            y = x[r].astype(F32) + conv_row(w2t[...], acts[at : at + 3 * c, :])
            block[done] = y
            control[done * c : (done + 1) * c, :] = y.astype(BF16)
            done += 1
    for r in range(done):
        residual[r] = jnp.dot(
            zt[...], control[r * c : (r + 1) * c, :], preferred_element_type=F32
        ).astype(BF16)


def mix_kernel(wanted, flags, block, arrived, *rest):
    whole, held, sem = rest[-3:]
    unet = flags[2:3, :1] > 0.5
    copies = []
    for r, to in enumerate(wanted):
        add = jnp.where(unet, arrived[r].astype(F32), 0.0)
        held[r] = (block[r] + add).astype(BF16)
        copies.append(pltpu.make_async_copy(held.at[r], whole.at[to], sem.at[r]))
        copies[-1].start()
    for copy in copies:
        copy.wait()


def mix(flags, block, arrived, wanted, whole, old):
    held = [] if old is None else [old]
    return pl.pallas_call(
        functools.partial(mix_kernel, wanted),
        out_shape=whole,
        in_specs=[VMEM, VMEM, VMEM] + [ANYWHERE] * len(held),
        out_specs=ANYWHERE,
        scratch_shapes=[
            pltpu.VMEM(arrived.shape, BF16),
            pltpu.SemaphoreType.DMA((len(wanted),)),
        ],
        input_output_aliases={3: 0} if held else {},
        compiler_params=pltpu.CompilerParams(vmem_limit_bytes=16 * 2**20),
        cost_estimate=pl.CostEstimate(flops=10**6, bytes_accessed=2**21, transcendentals=0),
        name="mix",
    )(flags, block, arrived, *held)


def on_device(feats, conv_first, conv_second, time_shift, norm_gains, zero_conv):
    strips = lax.axis_size("strip")
    flags = strip_flags(strips)
    x = jnp.transpose(feats[0], (0, 2, 1))
    rows, c, width = x.shape
    same_chip = [(i, i ^ 1) for i in range(strips)]
    next_chip = [(i, i + 1) for i in range(1, strips - 1, 2)]
    next_chip += [(target, source) for source, target in next_chip]
    shaped = jax.ShapeDtypeStruct
    stat = shaped((8, LANES), F32)
    wide = shaped((3 * c, 3 * c), BF16)
    halo = shaped((2, c, width), BF16)
    row_macs = 2 * 9 * c * c * width

    chips = [list(range(core, strips, 2)) for core in range(2)]

    def paired(st):
        return jnp.concatenate([st[:1], lax.ppermute(st[:1], "strip", same_chip)], axis=0)

    def spread(pair):
        sent = jnp.broadcast_to(pair[None], (strips // 2, 2, LANES))
        rows_of_all = lax.all_to_all(sent, "strip", 0, 0, axis_index_groups=chips)
        return rows_of_all.reshape(strips, LANES)

    st1, inner, outer = call(
        stats_kernel, "stats_first", 2, (stat, halo, halo), [], 16, 2 * 10**10
    )(flags, x)
    pair, inner, outer = lax.optimization_barrier((paired(st1), inner, outer))
    outer = lax.ppermute(outer, "strip", next_chip)
    inner = lax.ppermute(inner, "strip", same_chip)
    st1 = spread(pair)
    mid, st2, edges, w1t, w2t, zt, cols = call(
        first_kernel,
        "conv_first",
        10,
        (
            shaped((rows, c, width), F32),
            stat,
            shaped((6 * c, width), BF16),
            wide,
            wide,
            shaped((c, c), BF16),
            shaped((2 * c, LANES), F32),
        ),
        [pltpu.VMEM(((rows + 4) * c, width), BF16)],
        36,
        rows * row_macs,
    )(flags, x, inner, outer, st1, norm_gains[0], time_shift, conv_first[0], conv_second[0], zero_conv)
    st2 = spread(paired(st2))
    pieces = []
    after = zt
    for wanted in (((3, 5),), ((1, 3),), ((5, 7),), ((0, 1), (7, rows))):
        n = sum(end - begin for begin, end in wanted)
        block, residual = call(
            functools.partial(second_kernel, wanted),
            "conv_second",
            9,
            (shaped((n, c, width), F32), shaped((n, c, width), BF16)),
            [
                pltpu.VMEM(((n + 2 * len(wanted)) * c, width), BF16),
                pltpu.VMEM((n * c, width), BF16),
            ],
            32,
            n * row_macs,
            unread=1,
        )(flags, x, mid, st2, cols, w2t, zt, edges, w1t, after)
        after = residual
        listed = [r for begin, end in wanted for r in range(begin, end)]
        pieces.append((listed, block, lax.ppermute(residual, "branch", [(0, 1), (1, 0)])))
    whole = shaped((rows, c, width), BF16)
    out = None
    for listed, block, arrived in pieces:
        out = mix(flags, block, arrived, listed, whole, out)
    return jnp.transpose(out, (0, 2, 1))[None]


def solution(mesh):
    placed = (
        P("branch", "strip", None, None),
        P("branch", None, None, None, None),
        P("branch", None, None, None, None),
        P("branch", None),
        P("branch", None, None),
        P(),
    )
    return jax.shard_map(
        on_device,
        mesh=mesh,
        in_specs=placed,
        out_specs=P("branch", "strip", None, None),
        check_vma=False,
    )
```

```python
import functools

import jax
import jax.numpy as jnp
from jax import lax
from jax.experimental import pallas as pl
from jax.experimental.pallas import tpu as pltpu
from jax.sharding import PartitionSpec as P

G = 32
F32 = jnp.float32
BF16 = jnp.bfloat16
VMEM = pl.BlockSpec(memory_space=pltpu.VMEM)
ANYWHERE = pl.BlockSpec(memory_space=pl.ANY)
LANES = 128


def call(kernel, name, ins, outs, scratch, mib, flops, unread=0):
    return pl.pallas_call(
        kernel,
        out_shape=outs,
        in_specs=[VMEM] * ins + [ANYWHERE] * unread,
        out_specs=[VMEM] * len(outs),
        scratch_shapes=scratch,
        compiler_params=pltpu.CompilerParams(vmem_limit_bytes=mib * 2**20),
        cost_estimate=pl.CostEstimate(flops=flops, bytes_accessed=4 * 2**20, transcendentals=0),
        name=name,
    )


def group_masks(channels):
    per = channels // G
    ch = lax.broadcasted_iota(jnp.int32, (channels, LANES), 0)
    low = lax.broadcasted_iota(jnp.int32, (channels, LANES), 1) * per
    high = low - G * per
    first = jnp.where((ch >= low) & (ch < low + per), 1.0, 0.0)
    second = jnp.where((ch >= high) & (ch < high + per), 1.0, 0.0)
    return first, second


def column(row):
    n = row.shape[1]
    eye = lax.broadcasted_iota(jnp.int32, (n, n), 0) == lax.broadcasted_iota(jnp.int32, (n, n), 1)
    return jnp.sum(jnp.where(eye, row, 0.0), axis=1, keepdims=True)


def widened(v, width):
    return jnp.concatenate([v] * (width // LANES), axis=1)


def fold(x):
    parts = [x[:, i : i + LANES] for i in range(0, x.shape[1], LANES)]
    return functools.reduce(jnp.add, parts)


def strip_stats(load, rows, channels, width):
    first, second = group_masks(channels)
    count = rows * width * (channels // G)
    total = functools.reduce(jnp.add, [fold(load(r)) for r in range(rows)])
    total = jnp.sum(total, axis=1, keepdims=True)
    mean = jnp.sum(first * total, axis=0, keepdims=True) / count
    mean_c = jnp.sum(first * mean, axis=1, keepdims=True)
    squares = functools.reduce(
        jnp.add, [fold((load(r) - mean_c) * (load(r) - mean_c)) for r in range(rows)]
    )
    squares = jnp.sum(squares, axis=1, keepdims=True)
    return mean + jnp.sum(second * squares, axis=0, keepdims=True)


def whole_stats(stats, channels, count):
    first, second = group_masks(channels)
    strips = stats.shape[0]
    total = jnp.sum(stats, axis=0, keepdims=True)
    mean = total / strips
    off = stats - mean
    between = jnp.sum(off * off, axis=0, keepdims=True) * count
    mean_c = jnp.sum(first * mean, axis=1, keepdims=True)
    variance = jnp.sum(first * between + second * total, axis=1, keepdims=True) / (strips * count)
    return mean_c, lax.rsqrt(variance + 1e-5)


def silu_of_twice(half):
    return half + half * jnp.tanh(half)


def turned(w, out, kx):
    c = w.shape[2]
    out[kx * c : (kx + 1) * c, :] = jnp.concatenate([w[ky, kx].T for ky in range(3)], axis=1)


def conv_row(wt, rows):
    c, w = rows.shape[0] // 3, rows.shape[1]
    y = jnp.dot(wt, rows, preferred_element_type=F32)
    lane = lax.broadcasted_iota(jnp.int32, (c, w), 1)
    left = jnp.where(lane == 0, 0.0, pltpu.roll(y[:c], 1, 1))
    right = jnp.where(lane == w - 1, 0.0, pltpu.roll(y[2 * c :], w - 1, 1))
    return y[c : 2 * c] + left + right


def stats_kernel(flags, x, out):
    rows, c, width = x.shape
    st = strip_stats(lambda r: x[r].astype(F32), rows, c, width)
    out[...] = jnp.broadcast_to(st, out.shape)


def halo_kernel(flags, x, after, inner, outer):
    rows = x.shape[0]
    even = flags[3:4, :1] > 0.5
    for i in range(2):
        begin, end = x[i].astype(F32), x[rows - 2 + i].astype(F32)
        inner[i] = jnp.where(even, end, begin).astype(BF16)
        outer[i] = jnp.where(even, begin, end).astype(BF16)


def strip_flags(strips):
    here = lax.axis_index("strip")
    values = [here > 0, here < strips - 1, lax.axis_index("branch") == 1, here % 2 == 0]
    at = lax.broadcasted_iota(jnp.int32, (8, LANES), 0)
    return functools.reduce(
        jnp.add, [jnp.where((at == i) & v, 1.0, 0.0) for i, v in enumerate(values)]
    )


def first_kernel(
    flags, x, inner, outer, st, gains, shift, w1, mid, out, edges, w1t, cols, acts
):
    rows, c, width = x.shape
    mean, scale = whole_stats(st[...], c, rows * width * (c // G))
    scale = 0.5 * scale * column(gains[0:1, :])
    top, bottom = flags[0:1, :1], flags[1:2, :1]
    even = flags[3:4, :1] > 0.5

    def put(at):
        if at < 2:
            v, keep = jnp.where(even, outer[at].astype(F32), inner[at].astype(F32)), top
        elif at < rows + 2:
            v, keep = x[at - 2].astype(F32), None
        else:
            at_high = at - rows - 2
            v = jnp.where(even, inner[at_high].astype(F32), outer[at_high].astype(F32))
            keep = bottom
        a = silu_of_twice((v - mean) * scale)
        if keep is not None:
            a = a * keep
        a = a.astype(BF16)
        acts[at * c : (at + 1) * c, :] = a
        if at < 3:
            edges[at * c : (at + 1) * c, :] = a
        if at > rows:
            edges[(at - rows + 2) * c : (at - rows + 3) * c, :] = a

    for kx in range(3):
        turned(w1, w1t, kx)
    for at in (1, 2, 3):
        put(at)
    shift_c = column(shift[...])
    first, second = group_masks(c)
    per_row = width * (c // G)

    def keep_columns():
        both = jnp.concatenate([shift_c, column(gains[1:2, :])], axis=0)
        cols[...] = jnp.broadcast_to(both, cols.shape)

    beside = {1: keep_columns, 4: lambda: put(0), 6: lambda: put(rows + 3)}
    for r in range(1, rows + 1):
        y = conv_row(w1t[...], acts[r * c : (r + 3) * c, :]) + shift_c
        mid[r - 1] = y
        if r == 1:
            total = fold(y)
            row_sum = jnp.sum(first * jnp.sum(total, axis=1, keepdims=True), axis=0, keepdims=True)
            about = row_sum / per_row
            about_c = jnp.sum(first * about, axis=1, keepdims=True)
            squares = fold((y - about_c) * (y - about_c))
        else:
            total = total + fold(y)
            squares = squares + fold((y - about_c) * (y - about_c))
        if r < rows:
            put(r + 3)
        if r in beside:
            beside[r]()
    count = rows * per_row
    total = jnp.sum(total, axis=1, keepdims=True)
    squares = jnp.sum(squares, axis=1, keepdims=True)
    own_mean = jnp.sum(first * total, axis=0, keepdims=True) / count
    moved = (own_mean - about) * (own_mean - about) * count
    moved = pltpu.roll(jnp.broadcast_to(moved, (8, LANES)), G, 1)[:1]
    st2 = own_mean + jnp.sum(second * squares, axis=0, keepdims=True) - moved
    out[...] = jnp.broadcast_to(st2, out.shape)


def prepare_kernel(w2, z, after, w2t, zt):
    for kx in range(3):
        turned(w2, w2t, kx)
    zt[...] = z[...].T


def second_kernel(wanted, flags, x, mid, st, cols, w2t, zt, edges, w1t, after, *outs):
    block, residual, acts, control = outs
    rows, c, width = x.shape
    mean, scale = whole_stats(st[...], c, rows * width * (c // G))
    scale = scale * widened(0.5 * cols[c:, :], width)
    top, bottom = flags[0:1, :1], flags[1:2, :1]

    def put(at, slot):
        if at == 0:
            v = conv_row(w1t[...], edges[: 3 * c, :]) + widened(cols[:c, :], width)
        elif at == rows + 1:
            v = conv_row(w1t[...], edges[3 * c :, :]) + widened(cols[:c, :], width)
        else:
            v = mid[at - 1]
        a = silu_of_twice((v - mean) * scale)
        if at == 0:
            a = a * top
        if at == rows + 1:
            a = a * bottom
        acts[slot * c : (slot + 1) * c, :] = a.astype(BF16)

    done = 0
    slot = 0
    for begin, end in wanted:
        base = slot
        for at in range(begin, end + 2):
            put(at, slot)
            slot += 1
        for r in range(begin, end):
            at = (base + r - begin) * c
            y = x[r].astype(F32) + conv_row(w2t[...], acts[at : at + 3 * c, :])
            block[done] = y
            control[done * c : (done + 1) * c, :] = y.astype(BF16)
            done += 1
    for r in range(done):
        residual[r] = jnp.dot(
            zt[...], control[r * c : (r + 1) * c, :], preferred_element_type=F32
        ).astype(BF16)


def mix_kernel(wanted, flags, block, arrived, *rest):
    whole, held, sem = rest[-3:]
    unet = flags[2:3, :1] > 0.5
    copies = []
    for r, to in enumerate(wanted):
        add = jnp.where(unet, arrived[r].astype(F32), 0.0)
        held[r] = (block[r] + add).astype(BF16)
        copies.append(pltpu.make_async_copy(held.at[r], whole.at[to], sem.at[r]))
        copies[-1].start()
    for copy in copies:
        copy.wait()


def mix(flags, block, arrived, wanted, whole, old):
    held = [] if old is None else [old]
    return pl.pallas_call(
        functools.partial(mix_kernel, wanted),
        out_shape=whole,
        in_specs=[VMEM, VMEM, VMEM] + [ANYWHERE] * len(held),
        out_specs=ANYWHERE,
        scratch_shapes=[
            pltpu.VMEM(arrived.shape, BF16),
            pltpu.SemaphoreType.DMA((len(wanted),)),
        ],
        input_output_aliases={3: 0} if held else {},
        compiler_params=pltpu.CompilerParams(vmem_limit_bytes=16 * 2**20),
        cost_estimate=pl.CostEstimate(flops=10**6, bytes_accessed=2**21, transcendentals=0),
        name="mix",
    )(flags, block, arrived, *held)


def on_device(feats, conv_first, conv_second, time_shift, norm_gains, zero_conv):
    strips = lax.axis_size("strip")
    flags = strip_flags(strips)
    x = jnp.transpose(feats[0], (0, 2, 1))
    rows, c, width = x.shape
    same_chip = [(i, i ^ 1) for i in range(strips)]
    next_chip = [(i, i + 1) for i in range(1, strips - 1, 2)]
    next_chip += [(target, source) for source, target in next_chip]
    shaped = jax.ShapeDtypeStruct
    stat = shaped((8, LANES), F32)
    wide = shaped((3 * c, 3 * c), BF16)
    halo = shaped((2, c, width), BF16)
    row_macs = 2 * 9 * c * c * width

    chips = [list(range(core, strips, 2)) for core in range(2)]

    def paired(st):
        return jnp.concatenate([st[:1], lax.ppermute(st[:1], "strip", same_chip)], axis=0)

    def spread(pair):
        sent = jnp.broadcast_to(pair[None], (strips // 2, 2, LANES))
        rows_of_all = lax.all_to_all(sent, "strip", 0, 0, axis_index_groups=chips)
        return rows_of_all.reshape(strips, LANES)

    (st1,) = call(stats_kernel, "stats_first", 2, (stat,), [], 16, 2 * 10**10)(flags, x)
    inner, outer = call(halo_kernel, "halo", 2, (halo, halo), [], 16, 10**8, unread=1)(
        flags, x, st1
    )
    pair, inner, outer = lax.optimization_barrier((paired(st1), inner, outer))
    outer = lax.ppermute(outer, "strip", next_chip)
    inner = lax.ppermute(inner, "strip", same_chip)
    st1 = spread(pair)
    mid, st2, edges, w1t, cols = call(
        first_kernel,
        "conv_first",
        8,
        (
            shaped((rows, c, width), F32),
            stat,
            shaped((6 * c, width), BF16),
            wide,
            shaped((2 * c, LANES), F32),
        ),
        [pltpu.VMEM(((rows + 4) * c, width), BF16)],
        36,
        rows * row_macs,
    )(flags, x, inner, outer, st1, norm_gains[0], time_shift, conv_first[0])
    w2t, zt = call(
        prepare_kernel, "prepare", 2, (wide, shaped((c, c), BF16)), [], 16, 10**9, unread=1
    )(conv_second[0], zero_conv, st2)
    pair, w2t, zt = lax.optimization_barrier((paired(st2), w2t, zt))
    st2 = spread(pair)
    pieces = []
    after = zt
    for wanted in (((3, 5),), ((1, 3),), ((5, 7),), ((0, 1), (7, rows))):
        n = sum(end - begin for begin, end in wanted)
        block, residual = call(
            functools.partial(second_kernel, wanted),
            "conv_second",
            9,
            (shaped((n, c, width), F32), shaped((n, c, width), BF16)),
            [
                pltpu.VMEM(((n + 2 * len(wanted)) * c, width), BF16),
                pltpu.VMEM((n * c, width), BF16),
            ],
            32,
            n * row_macs,
            unread=1,
        )(flags, x, mid, st2, cols, w2t, zt, edges, w1t, after)
        after = residual
        listed = [r for begin, end in wanted for r in range(begin, end)]
        pieces.append((listed, block, lax.ppermute(residual, "branch", [(0, 1), (1, 0)])))
    whole = shaped((rows, c, width), BF16)
    out = None
    for listed, block, arrived in pieces:
        out = mix(flags, block, arrived, listed, whole, out)
    return jnp.transpose(out, (0, 2, 1))[None]


def solution(mesh):
    placed = (
        P("branch", "strip", None, None),
        P("branch", None, None, None, None),
        P("branch", None, None, None, None),
        P("branch", None),
        P("branch", None, None),
        P(),
    )
    return jax.shard_map(
        on_device,
        mesh=mesh,
        in_specs=placed,
        out_specs=P("branch", "strip", None, None),
        check_vma=False,
    )
```

```python
import functools

import jax
import jax.numpy as jnp
from jax import lax
from jax.experimental import pallas as pl
from jax.experimental.pallas import tpu as pltpu
from jax.sharding import PartitionSpec as P

G = 32
F32 = jnp.float32
BF16 = jnp.bfloat16
VMEM = pl.BlockSpec(memory_space=pltpu.VMEM)
ANYWHERE = pl.BlockSpec(memory_space=pl.ANY)
LANES = 128


def call(kernel, name, ins, outs, scratch, mib, flops, unread=0):
    return pl.pallas_call(
        kernel,
        out_shape=outs,
        in_specs=[VMEM] * ins + [ANYWHERE] * unread,
        out_specs=[VMEM] * len(outs),
        scratch_shapes=scratch,
        compiler_params=pltpu.CompilerParams(vmem_limit_bytes=mib * 2**20),
        cost_estimate=pl.CostEstimate(flops=flops, bytes_accessed=4 * 2**20, transcendentals=0),
        name=name,
    )


def group_masks(channels):
    per = channels // G
    ch = lax.broadcasted_iota(jnp.int32, (channels, LANES), 0)
    low = lax.broadcasted_iota(jnp.int32, (channels, LANES), 1) * per
    high = low - G * per
    first = jnp.where((ch >= low) & (ch < low + per), 1.0, 0.0)
    second = jnp.where((ch >= high) & (ch < high + per), 1.0, 0.0)
    return first, second


def column(row):
    n = row.shape[1]
    eye = lax.broadcasted_iota(jnp.int32, (n, n), 0) == lax.broadcasted_iota(jnp.int32, (n, n), 1)
    return jnp.sum(jnp.where(eye, row, 0.0), axis=1, keepdims=True)


def widened(v, width):
    return jnp.concatenate([v] * (width // LANES), axis=1)


def fold(x):
    parts = [x[:, i : i + LANES] for i in range(0, x.shape[1], LANES)]
    return functools.reduce(jnp.add, parts)


def strip_stats(load, rows, channels, width):
    first, second = group_masks(channels)
    count = rows * width * (channels // G)
    total = functools.reduce(jnp.add, [fold(load(r)) for r in range(rows)])
    total = jnp.sum(total, axis=1, keepdims=True)
    mean = jnp.sum(first * total, axis=0, keepdims=True) / count
    mean_c = jnp.sum(first * mean, axis=1, keepdims=True)
    squares = functools.reduce(
        jnp.add, [fold((load(r) - mean_c) * (load(r) - mean_c)) for r in range(rows)]
    )
    squares = jnp.sum(squares, axis=1, keepdims=True)
    return mean + jnp.sum(second * squares, axis=0, keepdims=True)


def whole_stats(stats, channels, count):
    first, second = group_masks(channels)
    strips = stats.shape[0]
    total = jnp.sum(stats, axis=0, keepdims=True)
    mean = total / strips
    off = stats - mean
    between = jnp.sum(off * off, axis=0, keepdims=True) * count
    mean_c = jnp.sum(first * mean, axis=1, keepdims=True)
    variance = jnp.sum(first * between + second * total, axis=1, keepdims=True) / (strips * count)
    return mean_c, lax.rsqrt(variance + 1e-5)


def silu_of_twice(half):
    return half + half * jnp.tanh(half)


def turned(w, out, kx):
    c = w.shape[2]
    out[kx * c : (kx + 1) * c, :] = jnp.concatenate([w[ky, kx].T for ky in range(3)], axis=1)


def conv_row(wt, rows):
    c, w = rows.shape[0] // 3, rows.shape[1]
    y = jnp.dot(wt, rows, preferred_element_type=F32)
    lane = lax.broadcasted_iota(jnp.int32, (c, w), 1)
    left = jnp.where(lane == 0, 0.0, pltpu.roll(y[:c], 1, 1))
    right = jnp.where(lane == w - 1, 0.0, pltpu.roll(y[2 * c :], w - 1, 1))
    return y[c : 2 * c] + left + right


def stats_kernel(flags, x, out):
    rows, c, width = x.shape
    st = strip_stats(lambda r: x[r].astype(F32), rows, c, width)
    out[...] = jnp.broadcast_to(st, out.shape)


def halo_kernel(flags, x, after, inner, outer):
    rows = x.shape[0]
    even = flags[3:4, :1] > 0.5
    for i in range(2):
        begin, end = x[i].astype(F32), x[rows - 2 + i].astype(F32)
        inner[i] = jnp.where(even, end, begin).astype(BF16)
        outer[i] = jnp.where(even, begin, end).astype(BF16)


def strip_flags(strips):
    here = lax.axis_index("strip")
    values = [here > 0, here < strips - 1, lax.axis_index("branch") == 1, here % 2 == 0]
    at = lax.broadcasted_iota(jnp.int32, (8, LANES), 0)
    return functools.reduce(
        jnp.add, [jnp.where((at == i) & v, 1.0, 0.0) for i, v in enumerate(values)]
    )


def first_kernel(
    flags, x, inner, outer, st, gains, shift, w1, mid, out, edges, w1t, cols, acts
):
    rows, c, width = x.shape
    mean, scale = whole_stats(st[...], c, rows * width * (c // G))
    scale = 0.5 * scale * column(gains[0:1, :])
    top, bottom = flags[0:1, :1], flags[1:2, :1]
    even = flags[3:4, :1] > 0.5

    def put(at):
        if at < 2:
            v, keep = jnp.where(even, outer[at].astype(F32), inner[at].astype(F32)), top
        elif at < rows + 2:
            v, keep = x[at - 2].astype(F32), None
        else:
            at_high = at - rows - 2
            v = jnp.where(even, inner[at_high].astype(F32), outer[at_high].astype(F32))
            keep = bottom
        a = silu_of_twice((v - mean) * scale)
        if keep is not None:
            a = a * keep
        a = a.astype(BF16)
        acts[at * c : (at + 1) * c, :] = a
        if at < 3:
            edges[at * c : (at + 1) * c, :] = a
        if at > rows:
            edges[(at - rows + 2) * c : (at - rows + 3) * c, :] = a

    for kx in range(3):
        turned(w1, w1t, kx)
    for at in (1, 2, 3):
        put(at)
    shift_c = column(shift[...])
    first, second = group_masks(c)
    per_row = width * (c // G)

    def keep_columns():
        both = jnp.concatenate([shift_c, column(gains[1:2, :])], axis=0)
        cols[...] = jnp.broadcast_to(both, cols.shape)

    beside = {1: keep_columns, 4: lambda: put(0), 6: lambda: put(rows + 3)}
    for r in range(1, rows + 1):
        y = conv_row(w1t[...], acts[r * c : (r + 3) * c, :]) + shift_c
        mid[r - 1] = y
        if r == 1:
            total = fold(y)
            row_sum = jnp.sum(first * jnp.sum(total, axis=1, keepdims=True), axis=0, keepdims=True)
            about = row_sum / per_row
            about_c = jnp.sum(first * about, axis=1, keepdims=True)
            squares = fold((y - about_c) * (y - about_c))
        else:
            total = total + fold(y)
            squares = squares + fold((y - about_c) * (y - about_c))
        if r < rows:
            put(r + 3)
        if r in beside:
            beside[r]()
    count = rows * per_row
    total = jnp.sum(total, axis=1, keepdims=True)
    squares = jnp.sum(squares, axis=1, keepdims=True)
    own_mean = jnp.sum(first * total, axis=0, keepdims=True) / count
    moved = (own_mean - about) * (own_mean - about) * count
    moved = pltpu.roll(jnp.broadcast_to(moved, (8, LANES)), G, 1)[:1]
    st2 = own_mean + jnp.sum(second * squares, axis=0, keepdims=True) - moved
    out[...] = jnp.broadcast_to(st2, out.shape)


def prepare_kernel(w2, z, after, w2t, zt):
    for kx in range(3):
        turned(w2, w2t, kx)
    zt[...] = z[...].T


def second_kernel(wanted, flags, x, mid, st, cols, w2t, zt, edges, w1t, after, *outs):
    block, residual, acts, control = outs
    rows, c, width = x.shape
    mean, scale = whole_stats(st[...], c, rows * width * (c // G))
    scale = scale * widened(0.5 * cols[c:, :], width)
    top, bottom = flags[0:1, :1], flags[1:2, :1]

    def put(at, slot):
        if at == 0:
            v = conv_row(w1t[...], edges[: 3 * c, :]) + widened(cols[:c, :], width)
        elif at == rows + 1:
            v = conv_row(w1t[...], edges[3 * c :, :]) + widened(cols[:c, :], width)
        else:
            v = mid[at - 1]
        a = silu_of_twice((v - mean) * scale)
        if at == 0:
            a = a * top
        if at == rows + 1:
            a = a * bottom
        acts[slot * c : (slot + 1) * c, :] = a.astype(BF16)

    done = 0
    slot = 0
    for begin, end in wanted:
        base = slot
        for at in range(begin, end + 2):
            put(at, slot)
            slot += 1
        for r in range(begin, end):
            at = (base + r - begin) * c
            y = x[r].astype(F32) + conv_row(w2t[...], acts[at : at + 3 * c, :])
            block[done] = y
            control[done * c : (done + 1) * c, :] = y.astype(BF16)
            done += 1
    for r in range(done):
        residual[r] = jnp.dot(
            zt[...], control[r * c : (r + 1) * c, :], preferred_element_type=F32
        ).astype(BF16)


def mix_kernel(wanted, flags, block, arrived, *rest):
    whole, held, sem = rest[-3:]
    unet = flags[2:3, :1] > 0.5
    copies = []
    for r, to in enumerate(wanted):
        add = jnp.where(unet, arrived[r].astype(F32), 0.0)
        held[r] = (block[r] + add).astype(BF16)
        copies.append(pltpu.make_async_copy(held.at[r], whole.at[to], sem.at[r]))
        copies[-1].start()
    for copy in copies:
        copy.wait()


def mix(flags, block, arrived, wanted, whole, old):
    held = [] if old is None else [old]
    return pl.pallas_call(
        functools.partial(mix_kernel, wanted),
        out_shape=whole,
        in_specs=[VMEM, VMEM, VMEM] + [ANYWHERE] * len(held),
        out_specs=ANYWHERE,
        scratch_shapes=[
            pltpu.VMEM(arrived.shape, BF16),
            pltpu.SemaphoreType.DMA((len(wanted),)),
        ],
        input_output_aliases={3: 0} if held else {},
        compiler_params=pltpu.CompilerParams(vmem_limit_bytes=16 * 2**20),
        cost_estimate=pl.CostEstimate(flops=10**6, bytes_accessed=2**21, transcendentals=0),
        name="mix",
    )(flags, block, arrived, *held)


def on_device(feats, conv_first, conv_second, time_shift, norm_gains, zero_conv):
    strips = lax.axis_size("strip")
    flags = strip_flags(strips)
    x = jnp.transpose(feats[0], (0, 2, 1))
    rows, c, width = x.shape
    same_chip = [(i, i ^ 1) for i in range(strips)]
    next_chip = [(i, i + 1) for i in range(1, strips - 1, 2)]
    next_chip += [(target, source) for source, target in next_chip]
    shaped = jax.ShapeDtypeStruct
    stat = shaped((8, LANES), F32)
    wide = shaped((3 * c, 3 * c), BF16)
    halo = shaped((2, c, width), BF16)
    row_macs = 2 * 9 * c * c * width

    chips = [list(range(core, strips, 2)) for core in range(2)]

    def paired(st):
        return jnp.concatenate([st[:1], lax.ppermute(st[:1], "strip", same_chip)], axis=0)

    def spread(pair):
        sent = jnp.broadcast_to(pair[None], (strips // 2, 2, LANES))
        rows_of_all = lax.all_to_all(sent, "strip", 0, 0, axis_index_groups=chips)
        return rows_of_all.reshape(strips, LANES)

    (st1,) = call(stats_kernel, "stats_first", 2, (stat,), [], 16, 2 * 10**10)(flags, x)
    inner, outer = call(halo_kernel, "halo", 2, (halo, halo), [], 16, 10**8, unread=1)(
        flags, x, st1
    )
    pair, inner = lax.optimization_barrier((paired(st1), inner))
    outer = lax.ppermute(outer, "strip", next_chip)
    inner = lax.ppermute(inner, "strip", same_chip)
    st1 = spread(pair)
    mid, st2, edges, w1t, cols = call(
        first_kernel,
        "conv_first",
        8,
        (
            shaped((rows, c, width), F32),
            stat,
            shaped((6 * c, width), BF16),
            wide,
            shaped((2 * c, LANES), F32),
        ),
        [pltpu.VMEM(((rows + 4) * c, width), BF16)],
        36,
        rows * row_macs,
    )(flags, x, inner, outer, st1, norm_gains[0], time_shift, conv_first[0])
    w2t, zt = call(
        prepare_kernel, "prepare", 2, (wide, shaped((c, c), BF16)), [], 16, 10**9, unread=1
    )(conv_second[0], zero_conv, st2)
    pair, w2t, zt = lax.optimization_barrier((paired(st2), w2t, zt))
    st2 = spread(pair)
    pieces = []
    after = zt
    for wanted in (((3, 5),), ((1, 3),), ((5, 7),), ((0, 1), (7, rows))):
        n = sum(end - begin for begin, end in wanted)
        block, residual = call(
            functools.partial(second_kernel, wanted),
            "conv_second",
            9,
            (shaped((n, c, width), F32), shaped((n, c, width), BF16)),
            [
                pltpu.VMEM(((n + 2 * len(wanted)) * c, width), BF16),
                pltpu.VMEM((n * c, width), BF16),
            ],
            32,
            n * row_macs,
            unread=1,
        )(flags, x, mid, st2, cols, w2t, zt, edges, w1t, after)
        after = residual
        listed = [r for begin, end in wanted for r in range(begin, end)]
        pieces.append((listed, block, lax.ppermute(residual, "branch", [(0, 1), (1, 0)])))
    whole = shaped((rows, c, width), BF16)
    out = None
    for listed, block, arrived in pieces:
        out = mix(flags, block, arrived, listed, whole, out)
    return jnp.transpose(out, (0, 2, 1))[None]


def solution(mesh):
    placed = (
        P("branch", "strip", None, None),
        P("branch", None, None, None, None),
        P("branch", None, None, None, None),
        P("branch", None),
        P("branch", None, None),
        P(),
    )
    return jax.shard_map(
        on_device,
        mesh=mesh,
        in_specs=placed,
        out_specs=P("branch", "strip", None, None),
        check_vma=False,
    )
```

```python
import functools

import jax
import jax.numpy as jnp
from jax import lax
from jax.experimental import pallas as pl
from jax.experimental.pallas import tpu as pltpu
from jax.sharding import PartitionSpec as P

G = 32
F32 = jnp.float32
BF16 = jnp.bfloat16
VMEM = pl.BlockSpec(memory_space=pltpu.VMEM)
ANYWHERE = pl.BlockSpec(memory_space=pl.ANY)
LANES = 128


def call(kernel, name, ins, outs, scratch, mib, flops, unread=0):
    return pl.pallas_call(
        kernel,
        out_shape=outs,
        in_specs=[VMEM] * ins + [ANYWHERE] * unread,
        out_specs=[VMEM] * len(outs),
        scratch_shapes=scratch,
        compiler_params=pltpu.CompilerParams(vmem_limit_bytes=mib * 2**20),
        cost_estimate=pl.CostEstimate(flops=flops, bytes_accessed=4 * 2**20, transcendentals=0),
        name=name,
    )


def group_masks(channels):
    per = channels // G
    ch = lax.broadcasted_iota(jnp.int32, (channels, LANES), 0)
    low = lax.broadcasted_iota(jnp.int32, (channels, LANES), 1) * per
    high = low - G * per
    first = jnp.where((ch >= low) & (ch < low + per), 1.0, 0.0)
    second = jnp.where((ch >= high) & (ch < high + per), 1.0, 0.0)
    return first, second


def column(row):
    n = row.shape[1]
    eye = lax.broadcasted_iota(jnp.int32, (n, n), 0) == lax.broadcasted_iota(jnp.int32, (n, n), 1)
    return jnp.sum(jnp.where(eye, row, 0.0), axis=1, keepdims=True)


def widened(v, width):
    return jnp.concatenate([v] * (width // LANES), axis=1)


def fold(x):
    parts = [x[:, i : i + LANES] for i in range(0, x.shape[1], LANES)]
    return functools.reduce(jnp.add, parts)


def strip_stats(load, rows, channels, width):
    first, second = group_masks(channels)
    count = rows * width * (channels // G)
    total = functools.reduce(jnp.add, [fold(load(r)) for r in range(rows)])
    total = jnp.sum(total, axis=1, keepdims=True)
    mean = jnp.sum(first * total, axis=0, keepdims=True) / count
    mean_c = jnp.sum(first * mean, axis=1, keepdims=True)
    squares = functools.reduce(
        jnp.add, [fold((load(r) - mean_c) * (load(r) - mean_c)) for r in range(rows)]
    )
    squares = jnp.sum(squares, axis=1, keepdims=True)
    return mean + jnp.sum(second * squares, axis=0, keepdims=True)


def whole_stats(stats, channels, count):
    first, second = group_masks(channels)
    strips = stats.shape[0]
    total = jnp.sum(stats, axis=0, keepdims=True)
    mean = total / strips
    off = stats - mean
    between = jnp.sum(off * off, axis=0, keepdims=True) * count
    mean_c = jnp.sum(first * mean, axis=1, keepdims=True)
    variance = jnp.sum(first * between + second * total, axis=1, keepdims=True) / (strips * count)
    return mean_c, lax.rsqrt(variance + 1e-5)


def silu_of_twice(half):
    return half + half * jnp.tanh(half)


def turned(w, out, kx):
    c = w.shape[2]
    out[kx * c : (kx + 1) * c, :] = jnp.concatenate([w[ky, kx].T for ky in range(3)], axis=1)


def conv_row(wt, rows):
    c, w = rows.shape[0] // 3, rows.shape[1]
    y = jnp.dot(wt, rows, preferred_element_type=F32)
    lane = lax.broadcasted_iota(jnp.int32, (c, w), 1)
    left = jnp.where(lane == 0, 0.0, pltpu.roll(y[:c], 1, 1))
    right = jnp.where(lane == w - 1, 0.0, pltpu.roll(y[2 * c :], w - 1, 1))
    return y[c : 2 * c] + left + right


def stats_kernel(flags, x, out):
    rows, c, width = x.shape
    st = strip_stats(lambda r: x[r].astype(F32), rows, c, width)
    out[...] = jnp.broadcast_to(st, out.shape)


def halo_kernel(flags, x, after, inner, outer):
    rows = x.shape[0]
    even = flags[3:4, :1] > 0.5
    for i in range(2):
        begin, end = x[i].astype(F32), x[rows - 2 + i].astype(F32)
        inner[i] = jnp.where(even, end, begin).astype(BF16)
        outer[i] = jnp.where(even, begin, end).astype(BF16)


def strip_flags(strips):
    here = lax.axis_index("strip")
    values = [here > 0, here < strips - 1, lax.axis_index("branch") == 1, here % 2 == 0]
    at = lax.broadcasted_iota(jnp.int32, (8, LANES), 0)
    return functools.reduce(
        jnp.add, [jnp.where((at == i) & v, 1.0, 0.0) for i, v in enumerate(values)]
    )


def first_row(flags, x, inner, outer, mean, scale, at):
    rows = x.shape[0]
    even = flags[3:4, :1] > 0.5
    keep = None
    if at < 2:
        v = jnp.where(even, outer[at].astype(F32), inner[at].astype(F32))
        keep = flags[0:1, :1]
    elif at < rows + 2:
        v = x[at - 2].astype(F32)
    else:
        at_high = at - rows - 2
        v = jnp.where(even, inner[at_high].astype(F32), outer[at_high].astype(F32))
        keep = flags[1:2, :1]
    a = silu_of_twice((v - mean) * scale)
    if keep is not None:
        a = a * keep
    return a.astype(BF16)


def first_kernel(
    flags, x, inner, outer, st, gains, shift, w1, mid, out, w1t, cols, acts
):
    rows, c, width = x.shape
    mean, scale = whole_stats(st[...], c, rows * width * (c // G))
    scale = 0.5 * scale * column(gains[0:1, :])
    top, bottom = flags[0:1, :1], flags[1:2, :1]

    def put(at):
        acts[at * c : (at + 1) * c, :] = first_row(flags, x, inner, outer, mean, scale, at)

    for kx in range(3):
        turned(w1, w1t, kx)
    for at in (1, 2, 3):
        put(at)
    shift_c = column(shift[...])
    first, second = group_masks(c)
    per_row = width * (c // G)

    def keep_columns():
        both = jnp.concatenate([shift_c, column(gains[1:2, :])], axis=0)
        cols[...] = jnp.broadcast_to(both, cols.shape)

    beside = {1: keep_columns}
    for r in range(1, rows + 1):
        y = conv_row(w1t[...], acts[r * c : (r + 3) * c, :]) + shift_c
        mid[r - 1] = y
        if r == 1:
            total = fold(y)
            row_sum = jnp.sum(first * jnp.sum(total, axis=1, keepdims=True), axis=0, keepdims=True)
            about = row_sum / per_row
            about_c = jnp.sum(first * about, axis=1, keepdims=True)
            squares = fold((y - about_c) * (y - about_c))
        else:
            total = total + fold(y)
            squares = squares + fold((y - about_c) * (y - about_c))
        if r < rows:
            put(r + 3)
        if r in beside:
            beside[r]()
    count = rows * per_row
    total = jnp.sum(total, axis=1, keepdims=True)
    squares = jnp.sum(squares, axis=1, keepdims=True)
    own_mean = jnp.sum(first * total, axis=0, keepdims=True) / count
    moved = (own_mean - about) * (own_mean - about) * count
    moved = pltpu.roll(jnp.broadcast_to(moved, (8, LANES)), G, 1)[:1]
    st2 = own_mean + jnp.sum(second * squares, axis=0, keepdims=True) - moved
    out[...] = jnp.broadcast_to(st2, out.shape)


def prepare_kernel(w2, z, after, w2t, zt):
    for kx in range(3):
        turned(w2, w2t, kx)
    zt[...] = z[...].T


def second_kernel(
    wanted, flags, x, mid, st, cols, w2t, zt, inner, outer, st1, gains, w1t, after, *outs
):
    block, residual, acts, control, edges = outs
    rows, c, width = x.shape
    mean, scale = whole_stats(st[...], c, rows * width * (c // G))
    scale = scale * widened(0.5 * cols[c:, :], width)
    top, bottom = flags[0:1, :1], flags[1:2, :1]

    if any(begin == 0 or end == rows for begin, end in wanted):
        mean_one, scale_one = whole_stats(st1[...], c, rows * width * (c // G))
        scale_one = 0.5 * scale_one * column(gains[0:1, :])

    def edge_row(begin):
        for i in range(3):
            edges[i * c : (i + 1) * c, :] = first_row(
                flags, x, inner, outer, mean_one, scale_one, begin + i
            )
        return conv_row(w1t[...], edges[...]) + widened(cols[:c, :], width)

    def put(at, slot):
        if at == 0 or at == rows + 1:
            v = edge_row(at)
        else:
            v = mid[at - 1]
        a = silu_of_twice((v - mean) * scale)
        if at == 0:
            a = a * top
        if at == rows + 1:
            a = a * bottom
        acts[slot * c : (slot + 1) * c, :] = a.astype(BF16)

    done = 0
    slot = 0
    for begin, end in wanted:
        base = slot
        for at in range(begin, end + 2):
            put(at, slot)
            slot += 1
        for r in range(begin, end):
            at = (base + r - begin) * c
            y = x[r].astype(F32) + conv_row(w2t[...], acts[at : at + 3 * c, :])
            block[done] = y
            control[done * c : (done + 1) * c, :] = y.astype(BF16)
            done += 1
    for r in range(done):
        residual[r] = jnp.dot(
            zt[...], control[r * c : (r + 1) * c, :], preferred_element_type=F32
        ).astype(BF16)


def mix_kernel(wanted, flags, block, arrived, *rest):
    whole, held, sem = rest[-3:]
    unet = flags[2:3, :1] > 0.5
    copies = []
    for r, to in enumerate(wanted):
        add = jnp.where(unet, arrived[r].astype(F32), 0.0)
        held[r] = (block[r] + add).astype(BF16)
        copies.append(pltpu.make_async_copy(held.at[r], whole.at[to], sem.at[r]))
        copies[-1].start()
    for copy in copies:
        copy.wait()


def mix(flags, block, arrived, wanted, whole, old):
    held = [] if old is None else [old]
    return pl.pallas_call(
        functools.partial(mix_kernel, wanted),
        out_shape=whole,
        in_specs=[VMEM, VMEM, VMEM] + [ANYWHERE] * len(held),
        out_specs=ANYWHERE,
        scratch_shapes=[
            pltpu.VMEM(arrived.shape, BF16),
            pltpu.SemaphoreType.DMA((len(wanted),)),
        ],
        input_output_aliases={3: 0} if held else {},
        compiler_params=pltpu.CompilerParams(vmem_limit_bytes=16 * 2**20),
        cost_estimate=pl.CostEstimate(flops=10**6, bytes_accessed=2**21, transcendentals=0),
        name="mix",
    )(flags, block, arrived, *held)


def on_device(feats, conv_first, conv_second, time_shift, norm_gains, zero_conv):
    strips = lax.axis_size("strip")
    flags = strip_flags(strips)
    x = jnp.transpose(feats[0], (0, 2, 1))
    rows, c, width = x.shape
    same_chip = [(i, i ^ 1) for i in range(strips)]
    next_chip = [(i, i + 1) for i in range(1, strips - 1, 2)]
    next_chip += [(target, source) for source, target in next_chip]
    shaped = jax.ShapeDtypeStruct
    stat = shaped((8, LANES), F32)
    wide = shaped((3 * c, 3 * c), BF16)
    halo = shaped((2, c, width), BF16)
    row_macs = 2 * 9 * c * c * width

    chips = [list(range(core, strips, 2)) for core in range(2)]

    def paired(st):
        return jnp.concatenate([st[:1], lax.ppermute(st[:1], "strip", same_chip)], axis=0)

    def spread(pair):
        sent = jnp.broadcast_to(pair[None], (strips // 2, 2, LANES))
        rows_of_all = lax.all_to_all(sent, "strip", 0, 0, axis_index_groups=chips)
        return rows_of_all.reshape(strips, LANES)

    (st1,) = call(stats_kernel, "stats_first", 2, (stat,), [], 16, 2 * 10**10)(flags, x)
    inner, outer = call(halo_kernel, "halo", 2, (halo, halo), [], 16, 10**8, unread=1)(
        flags, x, st1
    )
    pair, inner = lax.optimization_barrier((paired(st1), inner))
    outer = lax.ppermute(outer, "strip", next_chip)
    inner = lax.ppermute(inner, "strip", same_chip)
    st1 = spread(pair)
    mid, st2, w1t, cols = call(
        first_kernel,
        "conv_first",
        8,
        (
            shaped((rows, c, width), F32),
            stat,
            wide,
            shaped((2 * c, LANES), F32),
        ),
        [pltpu.VMEM(((rows + 4) * c, width), BF16)],
        36,
        rows * row_macs,
    )(flags, x, inner, outer, st1, norm_gains[0], time_shift, conv_first[0])
    w2t, zt = call(
        prepare_kernel, "prepare", 2, (wide, shaped((c, c), BF16)), [], 16, 10**9, unread=1
    )(conv_second[0], zero_conv, st2)
    pair, w2t, zt = lax.optimization_barrier((paired(st2), w2t, zt))
    st2 = spread(pair)
    pieces = []
    after = zt
    for wanted in (((3, 5),), ((1, 3),), ((5, 7),), ((0, 1), (7, rows))):
        n = sum(end - begin for begin, end in wanted)
        block, residual = call(
            functools.partial(second_kernel, wanted),
            "conv_second",
            12,
            (shaped((n, c, width), F32), shaped((n, c, width), BF16)),
            [
                pltpu.VMEM(((n + 2 * len(wanted)) * c, width), BF16),
                pltpu.VMEM((n * c, width), BF16),
                pltpu.VMEM((3 * c, width), BF16),
            ],
            32,
            n * row_macs,
            unread=1,
        )(flags, x, mid, st2, cols, w2t, zt, inner, outer, st1, norm_gains[0], w1t, after)
        after = residual
        listed = [r for begin, end in wanted for r in range(begin, end)]
        pieces.append((listed, block, lax.ppermute(residual, "branch", [(0, 1), (1, 0)])))
    whole = shaped((rows, c, width), BF16)
    out = None
    for listed, block, arrived in pieces:
        out = mix(flags, block, arrived, listed, whole, out)
    return jnp.transpose(out, (0, 2, 1))[None]


def solution(mesh):
    placed = (
        P("branch", "strip", None, None),
        P("branch", None, None, None, None),
        P("branch", None, None, None, None),
        P("branch", None),
        P("branch", None, None),
        P(),
    )
    return jax.shard_map(
        on_device,
        mesh=mesh,
        in_specs=placed,
        out_specs=P("branch", "strip", None, None),
        check_vma=False,
    )
```

```python
import functools

import jax
import jax.numpy as jnp
from jax import lax
from jax.experimental import pallas as pl
from jax.experimental.pallas import tpu as pltpu
from jax.sharding import PartitionSpec as P

G = 32
F32 = jnp.float32
BF16 = jnp.bfloat16
VMEM = pl.BlockSpec(memory_space=pltpu.VMEM)
ANYWHERE = pl.BlockSpec(memory_space=pl.ANY)
LANES = 128


def call(kernel, name, ins, outs, scratch, mib, flops, unread=0):
    return pl.pallas_call(
        kernel,
        out_shape=outs,
        in_specs=[VMEM] * ins + [ANYWHERE] * unread,
        out_specs=[VMEM] * len(outs),
        scratch_shapes=scratch,
        compiler_params=pltpu.CompilerParams(vmem_limit_bytes=mib * 2**20),
        cost_estimate=pl.CostEstimate(flops=flops, bytes_accessed=4 * 2**20, transcendentals=0),
        name=name,
    )


def group_masks(channels):
    per = channels // G
    ch = lax.broadcasted_iota(jnp.int32, (channels, LANES), 0)
    low = lax.broadcasted_iota(jnp.int32, (channels, LANES), 1) * per
    high = low - G * per
    first = jnp.where((ch >= low) & (ch < low + per), 1.0, 0.0)
    second = jnp.where((ch >= high) & (ch < high + per), 1.0, 0.0)
    return first, second


def column(row):
    n = row.shape[1]
    eye = lax.broadcasted_iota(jnp.int32, (n, n), 0) == lax.broadcasted_iota(jnp.int32, (n, n), 1)
    return jnp.sum(jnp.where(eye, row, 0.0), axis=1, keepdims=True)


def widened(v, width):
    return jnp.concatenate([v] * (width // LANES), axis=1)


def fold(x):
    parts = [x[:, i : i + LANES] for i in range(0, x.shape[1], LANES)]
    return functools.reduce(jnp.add, parts)


def strip_stats(load, rows, channels, width):
    first, second = group_masks(channels)
    count = rows * width * (channels // G)
    total = functools.reduce(jnp.add, [fold(load(r)) for r in range(rows)])
    total = jnp.sum(total, axis=1, keepdims=True)
    mean = jnp.sum(first * total, axis=0, keepdims=True) / count
    mean_c = jnp.sum(first * mean, axis=1, keepdims=True)
    squares = functools.reduce(
        jnp.add, [fold((load(r) - mean_c) * (load(r) - mean_c)) for r in range(rows)]
    )
    squares = jnp.sum(squares, axis=1, keepdims=True)
    return mean + jnp.sum(second * squares, axis=0, keepdims=True)


def whole_stats(stats, channels, count):
    first, second = group_masks(channels)
    strips = stats.shape[0]
    total = jnp.sum(stats, axis=0, keepdims=True)
    mean = total / strips
    off = stats - mean
    between = jnp.sum(off * off, axis=0, keepdims=True) * count
    mean_c = jnp.sum(first * mean, axis=1, keepdims=True)
    variance = jnp.sum(first * between + second * total, axis=1, keepdims=True) / (strips * count)
    return mean_c, lax.rsqrt(variance + 1e-5)


def silu_of_twice(half):
    return half + half * jnp.tanh(half)


def turned(w, out, kx):
    c = w.shape[2]
    out[kx * c : (kx + 1) * c, :] = jnp.concatenate([w[ky, kx].T for ky in range(3)], axis=1)


def conv_row(wt, rows):
    c, w = rows.shape[0] // 3, rows.shape[1]
    y = jnp.dot(wt, rows, preferred_element_type=F32)
    lane = lax.broadcasted_iota(jnp.int32, (c, w), 1)
    left = jnp.where(lane == 0, 0.0, pltpu.roll(y[:c], 1, 1))
    right = jnp.where(lane == w - 1, 0.0, pltpu.roll(y[2 * c :], w - 1, 1))
    return y[c : 2 * c] + left + right


def stats_kernel(flags, x, out):
    rows, c, width = x.shape
    st = strip_stats(lambda r: x[r].astype(F32), rows, c, width)
    out[...] = jnp.broadcast_to(st, out.shape)


def halo_kernel(flags, x, after, inner, outer):
    rows = x.shape[0]
    even = flags[3:4, :1] > 0.5
    for i in range(2):
        begin, end = x[i].astype(F32), x[rows - 2 + i].astype(F32)
        inner[i] = jnp.where(even, end, begin).astype(BF16)
        outer[i] = jnp.where(even, begin, end).astype(BF16)


def strip_flags(strips):
    here = lax.axis_index("strip")
    values = [here > 0, here < strips - 1, lax.axis_index("branch") == 1, here % 2 == 0]
    at = lax.broadcasted_iota(jnp.int32, (8, LANES), 0)
    return functools.reduce(
        jnp.add, [jnp.where((at == i) & v, 1.0, 0.0) for i, v in enumerate(values)]
    )


def first_row(flags, x, inner, outer, mean, scale, at):
    rows = x.shape[0]
    even = flags[3:4, :1] > 0.5
    keep = None
    if at < 2:
        v = jnp.where(even, outer[at].astype(F32), inner[at].astype(F32))
        keep = flags[0:1, :1]
    elif at < rows + 2:
        v = x[at - 2].astype(F32)
    else:
        at_high = at - rows - 2
        v = jnp.where(even, inner[at_high].astype(F32), outer[at_high].astype(F32))
        keep = flags[1:2, :1]
    a = silu_of_twice((v - mean) * scale)
    if keep is not None:
        a = a * keep
    return a.astype(BF16)


def first_kernel(
    flags, x, inner, outer, st, gains, shift, w1, mid, out, w1t, cols, acts
):
    rows, c, width = x.shape
    mean, scale = whole_stats(st[...], c, rows * width * (c // G))
    scale = 0.5 * scale * column(gains[0:1, :])
    top, bottom = flags[0:1, :1], flags[1:2, :1]

    def put(at):
        acts[at * c : (at + 1) * c, :] = first_row(flags, x, inner, outer, mean, scale, at)

    for kx in range(3):
        turned(w1, w1t, kx)
    for at in (1, 2, 3):
        put(at)
    shift_c = column(shift[...])
    first, second = group_masks(c)
    per_row = width * (c // G)

    def keep_columns():
        both = jnp.concatenate([shift_c, column(gains[1:2, :])], axis=0)
        cols[...] = jnp.broadcast_to(both, cols.shape)

    beside = {1: keep_columns}
    for r in range(1, rows + 1):
        y = conv_row(w1t[...], acts[r * c : (r + 3) * c, :]) + shift_c
        mid[r - 1] = y
        if r == 1:
            total = fold(y)
            row_sum = jnp.sum(first * jnp.sum(total, axis=1, keepdims=True), axis=0, keepdims=True)
            about = row_sum / per_row
            about_c = jnp.sum(first * about, axis=1, keepdims=True)
            squares = fold((y - about_c) * (y - about_c))
        else:
            total = total + fold(y)
            squares = squares + fold((y - about_c) * (y - about_c))
        if r < rows:
            put(r + 3)
        if r in beside:
            beside[r]()
    count = rows * per_row
    total = jnp.sum(total, axis=1, keepdims=True)
    squares = jnp.sum(squares, axis=1, keepdims=True)
    own_mean = jnp.sum(first * total, axis=0, keepdims=True) / count
    moved = (own_mean - about) * (own_mean - about) * count
    moved = pltpu.roll(jnp.broadcast_to(moved, (8, LANES)), G, 1)[:1]
    st2 = own_mean + jnp.sum(second * squares, axis=0, keepdims=True) - moved
    out[...] = jnp.broadcast_to(st2, out.shape)


def prepare_kernel(w2, z, after, w2t, zt):
    for kx in range(3):
        turned(w2, w2t, kx)
    zt[...] = z[...].T


def second_kernel(
    wanted, flags, x, mid, st, cols, w2t, zt, inner, outer, st1, gains, w1t, after, *outs
):
    block, residual, acts, control, edges = outs
    rows, c, width = x.shape
    mean, scale = whole_stats(st[...], c, rows * width * (c // G))
    scale = scale * widened(0.5 * cols[c:, :], width)
    top, bottom = flags[0:1, :1], flags[1:2, :1]

    if any(begin == 0 or end == rows for begin, end in wanted):
        mean_one, scale_one = whole_stats(st1[...], c, rows * width * (c // G))
        scale_one = 0.5 * scale_one * column(gains[0:1, :])

    def edge_row(begin):
        for i in range(3):
            edges[i * c : (i + 1) * c, :] = first_row(
                flags, x, inner, outer, mean_one, scale_one, begin + i
            )
        return conv_row(w1t[...], edges[...]) + widened(cols[:c, :], width)

    def put(at, slot):
        if at == 0 or at == rows + 1:
            v = edge_row(at)
        else:
            v = mid[at - 1]
        a = silu_of_twice((v - mean) * scale)
        if at == 0:
            a = a * top
        if at == rows + 1:
            a = a * bottom
        acts[slot * c : (slot + 1) * c, :] = a.astype(BF16)

    done = 0
    slot = 0
    for begin, end in wanted:
        base = slot
        for at in range(begin, end + 2):
            put(at, slot)
            slot += 1
        for r in range(begin, end):
            at = (base + r - begin) * c
            y = x[r].astype(F32) + conv_row(w2t[...], acts[at : at + 3 * c, :])
            block[done] = y
            control[done * c : (done + 1) * c, :] = y.astype(BF16)
            done += 1
    for r in range(done):
        residual[r] = jnp.dot(
            zt[...], control[r * c : (r + 1) * c, :], preferred_element_type=F32
        ).astype(BF16)


def mix_kernel(wanted, flags, block, arrived, *rest):
    whole, held, sem = rest[-3:]
    unet = flags[2:3, :1] > 0.5
    copies = []
    for r, to in enumerate(wanted):
        add = jnp.where(unet, arrived[r].astype(F32), 0.0)
        held[r] = (block[r] + add).astype(BF16)
        copies.append(pltpu.make_async_copy(held.at[r], whole.at[to], sem.at[r]))
        copies[-1].start()
    for copy in copies:
        copy.wait()


def mix(flags, block, arrived, wanted, whole, old):
    held = [] if old is None else [old]
    return pl.pallas_call(
        functools.partial(mix_kernel, wanted),
        out_shape=whole,
        in_specs=[VMEM, VMEM, VMEM] + [ANYWHERE] * len(held),
        out_specs=ANYWHERE,
        scratch_shapes=[
            pltpu.VMEM(arrived.shape, BF16),
            pltpu.SemaphoreType.DMA((len(wanted),)),
        ],
        input_output_aliases={3: 0} if held else {},
        compiler_params=pltpu.CompilerParams(vmem_limit_bytes=16 * 2**20),
        cost_estimate=pl.CostEstimate(flops=10**6, bytes_accessed=2**21, transcendentals=0),
        name="mix",
    )(flags, block, arrived, *held)


def on_device(feats, conv_first, conv_second, time_shift, norm_gains, zero_conv):
    strips = lax.axis_size("strip")
    flags = strip_flags(strips)
    x = jnp.transpose(feats[0], (0, 2, 1))
    rows, c, width = x.shape
    same_chip = [(i, i ^ 1) for i in range(strips)]
    next_chip = [(i, i + 1) for i in range(1, strips - 1, 2)]
    next_chip += [(target, source) for source, target in next_chip]
    shaped = jax.ShapeDtypeStruct
    stat = shaped((8, LANES), F32)
    wide = shaped((3 * c, 3 * c), BF16)
    halo = shaped((2, c, width), BF16)
    row_macs = 2 * 9 * c * c * width

    chips = [list(range(core, strips, 2)) for core in range(2)]

    def paired(st):
        return jnp.concatenate([st[:1], lax.ppermute(st[:1], "strip", same_chip)], axis=0)

    def spread(pair):
        sent = jnp.broadcast_to(pair[None], (strips // 2, 2, LANES))
        rows_of_all = lax.all_to_all(sent, "strip", 0, 0, axis_index_groups=chips)
        return rows_of_all.reshape(strips, LANES)

    (st1,) = call(stats_kernel, "stats_first", 2, (stat,), [], 16, 2 * 10**10)(flags, x)
    inner, outer = call(halo_kernel, "halo", 2, (halo, halo), [], 16, 10**8, unread=1)(
        flags, x, st1
    )
    pair, inner = lax.optimization_barrier((paired(st1), inner))
    outer = lax.ppermute(outer, "strip", next_chip)
    inner = lax.ppermute(inner, "strip", same_chip)
    st1 = spread(pair)
    mid, st2, w1t, cols = call(
        first_kernel,
        "conv_first",
        8,
        (
            shaped((rows, c, width), F32),
            stat,
            wide,
            shaped((2 * c, LANES), F32),
        ),
        [pltpu.VMEM(((rows + 4) * c, width), BF16)],
        36,
        rows * row_macs,
    )(flags, x, inner, outer, st1, norm_gains[0], time_shift, conv_first[0])
    w2t, zt = call(
        prepare_kernel, "prepare", 2, (wide, shaped((c, c), BF16)), [], 16, 10**9, unread=1
    )(conv_second[0], zero_conv, st2)
    pair, w2t, zt = lax.optimization_barrier((paired(st2), w2t, zt))
    st2 = spread(pair)
    pieces = []
    after = zt
    for wanted in (((3, 5),), ((1, 3),), ((5, 7),), ((0, 1), (7, rows))):
        n = sum(end - begin for begin, end in wanted)
        block, residual = call(
            functools.partial(second_kernel, wanted),
            "conv_second",
            12,
            (shaped((n, c, width), F32), shaped((n, c, width), BF16)),
            [
                pltpu.VMEM(((n + 2 * len(wanted)) * c, width), BF16),
                pltpu.VMEM((n * c, width), BF16),
                pltpu.VMEM((3 * c, width), BF16),
            ],
            32,
            n * row_macs,
            unread=1,
        )(flags, x, mid, st2, cols, w2t, zt, inner, outer, st1, norm_gains[0], w1t, after)
        after = residual
        listed = [r for begin, end in wanted for r in range(begin, end)]
        route = [(0, 1)] if pieces else [(0, 1), (1, 0)]
        pieces.append((listed, block, lax.ppermute(residual, "branch", route)))
    whole = shaped((rows, c, width), BF16)
    out = None
    for listed, block, arrived in pieces:
        out = mix(flags, block, arrived, listed, whole, out)
    return jnp.transpose(out, (0, 2, 1))[None]


def solution(mesh):
    placed = (
        P("branch", "strip", None, None),
        P("branch", None, None, None, None),
        P("branch", None, None, None, None),
        P("branch", None),
        P("branch", None, None),
        P(),
    )
    return jax.shard_map(
        on_device,
        mesh=mesh,
        in_specs=placed,
        out_specs=P("branch", "strip", None, None),
        check_vma=False,
    )
```
